32 devices in a mesh: seq: 8 (over z, x), head: 4 (over y, core).
Axes of the slice: x: 2, y: 2, z: 4, core: 2. Of those that a mesh axis runs over, the one named last changes fastest.
Arguments:
- queries: bfloat16 [2048, 128], P('seq'), may hold values from -4 to 4
- keys: bfloat16 [2048, 128], P('seq'), may hold values from -4 to 4
- values: bfloat16 [2048, 2048], P('seq', 'head'), may hold values from -0.75 to 0.75
- level_codes: int32 [32, 12, 2048], P('head', None, 'seq'), may hold values from 1 to 15
- cotangent: bfloat16 [2048, 2048], P('seq', 'head'), may hold values from -0.75 to 0.75
Outputs:
- attended: bfloat16 [2048, 2048], P('seq', 'head')
- query_grad: float32 [2048, 128], P(('seq', 'head'))
- key_grad: float32 [2048, 128], P(('seq', 'head'))
- value_grad: bfloat16 [2048, 2048], P('seq', 'head')
The draws below stay inside these ranges and needn't reach their ends.
All inputs are finite; a program needn't handle non-finite values.
Results may differ from the reference program's by a relative error of at most 0.0057.
Values sent between devices are 32-bit elements; how exact they have to be, the bound alone decides.
A program may use at most 64 MiB of HBM per device.

```python
import jax
import jax.numpy as jnp
from jax import lax

DK = 128
HEADS = 32
P_SIZE = 64
STRETCH_BITS = 7
STRETCH = 128
TOKENS = 2048
LEVELS = 12
N_HEAD = 4


def touch_ends(entries, own_key, smallest, largest):
    longest = entries.shape.index(max(entries.shape))
    spots = []
    for shift in (0, 1):
        where = [jax.random.randint(jax.random.fold_in(own_key, axis), (), 0, length) for axis, length in enumerate(entries.shape)]
        where[longest] = (where[longest] + shift) % entries.shape[longest]
        spots.append(tuple(where))
    return entries.at[spots[0]].set(smallest).at[spots[1]].set(largest)


def shard_levels(key, dims, shards, smallest, largest):
    def one(dim, parts):
        steps = jax.random.uniform(jax.random.fold_in(jax.random.fold_in(key, 6), dim), (parts,), jnp.float32, smallest / len(shards), largest / len(shards))
        return jnp.repeat(jnp.exp(steps), dims[dim] // parts).reshape((-1,) + (1,) * (len(dims) - dim - 1))

    gain = one(*shards[0])
    for cut in shards[1:]:
        gain = gain * one(*cut)
    return gain


def scatter_about(stream_key, dims, deviation, reach, pieces=(), kind=jnp.bfloat16):
    level = shard_levels(stream_key, dims, pieces, -0.22, 0.18) if pieces else 1.0
    values = jax.random.normal(stream_key, dims, jnp.float32) * deviation * level
    return jnp.minimum(jnp.maximum(values, -reach), reach).astype(kind)


def setup_inputs(seed: int = 0) -> dict:
    streams_of = jax.random.split(jax.random.key(seed), 6)
    return {
        "queries": scatter_about(streams_of[0], (TOKENS, DK), 0.28, 4.0, ((0, 8),)),
        "keys": scatter_about(streams_of[1], (TOKENS, DK), 0.28, 4.0, ((0, 8),)),
        "values": scatter_about(streams_of[2], (TOKENS, HEADS * P_SIZE), 0.05, 0.75, ((0, 8), (1, 4))),
        "level_codes": touch_ends(jax.random.randint(streams_of[3], (HEADS, LEVELS, TOKENS), 1, 16), jax.random.fold_in(streams_of[3], 1), 1, 15).astype(jnp.int32),
        "cotangent": scatter_about(streams_of[4], (TOKENS, HEADS * P_SIZE), 0.05, 0.75, ((0, 8), (1, 4))),
    }


SCALE_CODE = 0.125


def round_trip(array):
    return lax.optimization_barrier(array.astype(jnp.bfloat16)).astype(jnp.float32)


def level_table(size):
    query_pos = lax.broadcasted_iota(jnp.int32, (size, size), 0)
    key_pos = lax.broadcasted_iota(jnp.int32, (size, size), 1)
    differ = jnp.bitwise_xor(query_pos, key_pos)
    depth = jnp.zeros((size, size), jnp.int32)
    for shift in range(size.bit_length() - 1):
        depth = depth + (jnp.right_shift(differ, shift) > 0).astype(jnp.int32)
    return depth, key_pos <= query_pos


def block_weights(weights_lvl, blocks):
    heads = weights_lvl.shape[0]
    depth, causal = level_table(STRETCH)
    total = jnp.zeros((blocks, heads, STRETCH, STRETCH), jnp.float32)
    for level in range(STRETCH_BITS + 1):
        factor = weights_lvl[:, level, :].reshape(heads, blocks, STRETCH).transpose(1, 0, 2)[:, :, :, None]
        total = total + jnp.where(jnp.logical_and(depth == level, causal), factor, 0.0)
    return total


def scale_heads(array, factor):
    tokens, total_width = array.shape
    heads = factor.shape[1]
    return (array.reshape(tokens, heads, total_width // heads) * factor[:, :, None]).reshape(tokens, total_width)


def group_pass(queries, keys, values, weights_lvl, cotangent):
    tokens, depth_width = queries.shape
    total_width = values.shape[1]
    heads = weights_lvl.shape[0]
    width = total_width // heads
    blocks = tokens // STRETCH
    span_bits = blocks.bit_length() - 1
    scale = depth_width ** -0.5
    base_level = STRETCH_BITS + 1
    query_float = queries.astype(jnp.float32)
    key_float = keys.astype(jnp.float32)
    value_float = values.astype(jnp.float32)
    grad_float = cotangent.astype(jnp.float32)
    query_blocks = query_float.reshape(blocks, STRETCH, depth_width)
    key_blocks = key_float.reshape(blocks, STRETCH, depth_width)
    value_heads = value_float.reshape(blocks, STRETCH, heads, width)
    grad_heads = grad_float.reshape(blocks, STRETCH, heads, width)
    scores = jnp.einsum("ntd,nsd->nts", query_blocks, key_blocks) * scale
    block_mask = block_weights(weights_lvl, blocks)
    mixed = round_trip(scores[:, None] * block_mask)
    attended = jnp.einsum("nhts,nshp->nthp", mixed, value_heads).reshape(tokens, total_width)
    value_grad = jnp.einsum("nhts,nthp->nshp", mixed, grad_heads).reshape(tokens, total_width)
    press = round_trip(jnp.einsum("nthp,nshp->nhts", grad_heads, value_heads) * block_mask)
    query_grad = jnp.einsum("nhts,nsd->ntd", press, key_blocks).reshape(tokens, depth_width) * scale
    key_grad = jnp.einsum("nhts,ntd->nsd", press, query_blocks).reshape(tokens, depth_width) * scale
    incoming = jnp.zeros((blocks, depth_width, total_width), jnp.float32)
    for step in range(span_bits):
        span = STRETCH * (2 ** step)
        groups = tokens // (2 * span)
        lower_keys = key_float.reshape(groups, 2, span, depth_width)[:, 0]
        lower_values = value_float.reshape(groups, 2, span, total_width)[:, 0]
        upper_queries = query_float.reshape(groups, 2, span, depth_width)[:, 1]
        upper_grad = grad_float.reshape(groups, 2, span, total_width)[:, 1]
        level_rows = weights_lvl[:, base_level + step, :].T.reshape(groups, 2, span, heads)[:, 1]
        level_rows = level_rows.reshape(groups * span, heads)
        state = round_trip(jnp.einsum("gmi,gmj->gij", lower_keys, lower_values))
        reading = jnp.einsum("gmi,gij->gmj", upper_queries, state) * scale
        reading = scale_heads(reading.reshape(groups * span, total_width), level_rows).reshape(groups, span, total_width)
        attended = attended + jnp.stack([jnp.zeros_like(reading), reading], axis=1).reshape(tokens, total_width)
        weighted = round_trip(scale_heads(upper_grad.reshape(groups * span, total_width), level_rows))
        weighted = weighted.reshape(groups, span, total_width)
        query_part = jnp.einsum("gmj,gij->gmi", weighted, state) * scale
        query_grad = query_grad + jnp.stack([jnp.zeros_like(query_part), query_part], axis=1).reshape(tokens, depth_width)
        sending = jnp.einsum("gmi,gmj->gij", upper_queries, weighted) * scale
        lower_blocks = span // STRETCH
        spread = jnp.broadcast_to(sending[:, None], (groups, lower_blocks, depth_width, total_width))
        incoming = incoming + jnp.stack([spread, jnp.zeros_like(spread)], axis=1).reshape(blocks, depth_width, total_width)
    incoming = round_trip(incoming)
    key_grad = key_grad + jnp.einsum("nsj,nij->nsi", value_float.reshape(blocks, STRETCH, total_width), incoming).reshape(tokens, depth_width)
    value_grad = value_grad + jnp.einsum("nsi,nij->nsj", key_blocks, incoming).reshape(tokens, total_width)
    return attended.astype(jnp.bfloat16), query_grad, key_grad, value_grad.astype(jnp.bfloat16)


def reference(queries, keys, values, level_codes, cotangent):
    group_heads = HEADS // N_HEAD
    group_width = group_heads * P_SIZE
    group_count = HEADS // group_heads

    def one_group(index):
        value_part = lax.dynamic_slice_in_dim(values, index * group_width, group_width, 1)
        grad_part = lax.dynamic_slice_in_dim(cotangent, index * group_width, group_width, 1)
        code_part = lax.dynamic_slice_in_dim(level_codes, index * group_heads, group_heads, 0)
        return group_pass(queries, keys, value_part, code_part.astype(jnp.float32) * SCALE_CODE, grad_part)

    attended, query_grad, key_grad, value_grad = lax.map(one_group, jnp.arange(group_count, dtype=jnp.int32))
    attended = attended.transpose(1, 0, 2).reshape(TOKENS, HEADS * P_SIZE)
    value_grad = value_grad.transpose(1, 0, 2).reshape(TOKENS, HEADS * P_SIZE)
    return attended, jnp.sum(query_grad, axis=0), jnp.sum(key_grad, axis=0), value_grad
```

```python
import functools

import jax
import jax.numpy as jnp
from jax import lax
from jax.experimental import pallas as pl
from jax.experimental.pallas import tpu as pltpu
from jax.sharding import PartitionSpec as P

STRETCH_BITS = 7
STRETCH = 128
LANES = 128
SCALE_CODE = 0.125
MESH = pl.DeviceIdType.MESH
PIECES = 8


def dot(a, b, da, db):
    return lax.dot_general(a, b, (((da,), (db,)), ((), ())), preferred_element_type=jnp.float32)


def kernel(
    n_seq, n_head,
    q_in, k_in, v_in, code_in, g_in,
    *rest,
):
    att_outs, vg_outs = rest[:PIECES], rest[PIECES:2 * PIECES]
    (
    qg_out, kg_out,
    att, vg, qg, kg, wts, lams, own, got, pend, back, racc, qk_send, qk_recv,
    f_send, f_recv, b_send, b_recv, h_send, h_recv,
    q_ref, k_ref, v_ref, code_ref, g_ref, load) = rest[2 * PIECES:]
    loads = [
        pltpu.make_async_copy(src, dst, load.at[i])
        for i, (src, dst) in enumerate((
            (k_in, k_ref), (v_in, v_ref), (g_in, g_ref), (q_in, q_ref), (code_in, code_ref)))
    ]
    for one in loads:
        one.start()
    tokens, depth = q_ref.shape
    total_width = v_ref.shape[1]
    heads = code_ref.shape[1]
    width = total_width // heads
    chunks = total_width // LANES
    per_chunk = LANES // width
    blocks = tokens // STRETCH
    rows = tokens // n_head
    bits = n_seq.bit_length() - 1
    scale = depth ** -0.5
    near = STRETCH_BITS + 1
    far = near + 1
    f32, bf16 = jnp.float32, jnp.bfloat16
    seq, head = lax.axis_index("seq"), lax.axis_index("head")
    bit = [lax.rem(lax.div(seq, 1 << b), 2) for b in range(bits)]
    low_bits = bits - 2
    top, mid = bits - 1, bits - 2
    stride = 1 << mid
    line = lax.div(seq, stride)
    partner = [seq + (1 << b) * (1 - 2 * bit[b]) for b in range(low_bits)]
    peers = [lax.rem(head + j, n_head) for j in range(1, n_head)]

    barrier = pltpu.get_barrier_semaphore()

    def greet(to):
        pl.semaphore_signal(barrier, inc=1, device_id=to, device_id_type=MESH)

    for b in range(low_bits):
        greet((partner[b], head))
    for peer in peers:
        greet((seq, peer))

    @pl.when(line > 0)
    def _():
        greet((seq - stride, head))

    @pl.when(line < 3)
    def _():
        greet((seq + stride, head))

    greetings = low_bits + n_head - 1 + (line > 0).astype(jnp.int32) + (line < 3).astype(jnp.int32)

    def forward(b, c, relay=False):
        return pltpu.make_async_remote_copy(
            src_ref=(got if relay else own).at[b, c], dst_ref=got.at[b, c],
            send_sem=f_send.at[b, c], recv_sem=f_recv.at[b, c],
            device_id=(partner[b] if b < low_bits else seq + stride, head), device_id_type=MESH)

    def backward(b, c):
        return pltpu.make_async_remote_copy(
            src_ref=pend.at[b, c], dst_ref=back.at[b, c],
            send_sem=b_send.at[b, c], recv_sem=b_recv.at[b, c],
            device_id=(partner[b] if b < low_bits else seq - stride, head), device_id_type=MESH)

    highest = [lax.div(seq, 2 << b) == (n_seq >> (b + 1)) - 1 for b in range(low_bits)]
    up_sends = [jnp.logical_or(bit[b] == 0, jnp.logical_not(highest[b])) for b in range(low_bits)]
    up_gets = [jnp.logical_or(bit[b] == 1, jnp.logical_not(highest[b])) for b in range(low_bits)]
    down_sends, down_gets = up_gets, up_sends

    cols = [slice(c * LANES, (c + 1) * LANES) for c in range(chunks)]

    spread = (
        lax.broadcasted_iota(jnp.int32, (heads, total_width), 1) // width
        == lax.broadcasted_iota(jnp.int32, (heads, total_width), 0)
    ).astype(f32)

    def level_weights(level):
        lam = code_ref[level].astype(f32) * SCALE_CODE
        return dot(lam, spread, 0, 0)

    def prepare(b):
        @pl.when(bit[b] == 1)
        def _():
            lam = level_weights(far + b)
            lams[b] = lam.astype(bf16)
            weighted = (g_ref[...].astype(f32) * lam).astype(bf16)
            wts[b] = weighted
            sending = dot(q_ref[...], weighted, 0, 0) * scale
            for c in range(chunks):
                pend[b, c] = sending[:, cols[c]]

        if b < low_bits:
            @pl.when(bit[b] == 0)
            def _():
                for c in range(chunks):
                    pend[b, c] = jnp.zeros((depth, LANES), f32)

    first_half = slice(0, STRETCH)
    second_half = slice(STRETCH, 2 * STRETCH)
    loads[0].wait()
    loads[1].wait()
    state_low = dot(k_ref[first_half, :], v_ref[first_half, :], 0, 0)
    state_all = state_low + dot(k_ref[second_half, :], v_ref[second_half, :], 0, 0)
    for c in range(chunks):
        own[0, c] = state_all[:, cols[c]]
    pl.semaphore_wait(barrier, greetings)
    for c in range(chunks):
        @pl.when(up_sends[0])
        def _(c=c):
            forward(0, c).start()
    for one in loads[2:]:
        one.wait()
    prepare(top)
    for c in range(chunks):
        @pl.when(line == 3)
        def _(c=c):
            backward(top, c).start()
    prepare(mid)
    for c in range(chunks):
        @pl.when(line == 3)
        def _(c=c):
            backward(mid, c).start()
    for b in range(low_bits - 1, -1, -1):
        prepare(b)

    key_pos = lax.rem(lax.broadcasted_iota(jnp.int32, (per_chunk * STRETCH, STRETCH), 0), STRETCH)
    query_pos = lax.broadcasted_iota(jnp.int32, (per_chunk * STRETCH, STRETCH), 1)
    differ = jnp.bitwise_xor(query_pos, key_pos)
    causal = key_pos <= query_pos
    lane_head = lax.broadcasted_iota(jnp.int32, (STRETCH, LANES), 1) // width

    def split_heads(block):
        block = block.astype(f32)
        return jnp.concatenate(
            [jnp.where(lane_head == i, block, 0.0) for i in range(per_chunk)], axis=0).astype(bf16)

    press_sum = [jnp.zeros((STRETCH, STRETCH), f32) for _ in range(blocks)]
    scores = []
    for n in range(blocks):
        at = slice(n * STRETCH, (n + 1) * STRETCH)
        one = dot(k_ref[at, :], q_ref[at, :], 1, 1) * scale
        scores.append(jnp.concatenate([one] * per_chunk, axis=0))

    def unit(n, c):
        at = slice(n * STRETCH, (n + 1) * STRETCH)

        def rows_of(level):
            parts = []
            for i in range(per_chunk):
                row = code_ref[level, c * per_chunk + i:c * per_chunk + i + 1, at].astype(f32) * SCALE_CODE
                parts.append(jnp.broadcast_to(row, (STRETCH, STRETCH)))
            return jnp.concatenate(parts, axis=0)

        mask = rows_of(STRETCH_BITS)
        for level in range(STRETCH_BITS - 1, -1, -1):
            mask = jnp.where(differ < (1 << level), rows_of(level), mask)
        mask = jnp.where(causal, mask, 0.0)
        mixed = (scores[n] * mask).astype(bf16)
        v_split = split_heads(v_ref[at, cols[c]])
        g_block = g_ref[at, cols[c]]
        att[at, cols[c]] = dot(mixed, v_split, 0, 0)
        wide = jnp.concatenate(
            [mixed[i * STRETCH:(i + 1) * STRETCH] for i in range(per_chunk)], axis=1)
        vg[at, cols[c]] = dot(wide, split_heads(g_block), 1, 0)
        press = dot(v_split, g_block, 1, 1) * mask
        for i in range(per_chunk):
            press_sum[n] = press_sum[n] + press[i * STRETCH:(i + 1) * STRETCH]

    def finish_block(n):
        at = slice(n * STRETCH, (n + 1) * STRETCH)
        press = press_sum[n].astype(bf16)
        qg[at, :] = dot(press, k_ref[at, :], 0, 0) * scale
        kg[at, :] = dot(press, q_ref[at, :], 1, 0) * scale

    def near_level():
        low = state_low.astype(bf16)
        lam = level_weights(near)[second_half]
        att[second_half, :] = att[second_half, :] + lam * (
            dot(q_ref[second_half, :], low, 1, 0) * scale)
        weighted = (g_ref[second_half, :].astype(f32) * lam).astype(bf16)
        qg[second_half, :] = qg[second_half, :] + dot(weighted, low, 1, 1) * scale
        return dot(q_ref[second_half, :], weighted, 0, 0) * scale

    def consume(b):
        @pl.when(bit[b] == 1)
        def _():
            total = jnp.zeros((tokens, depth), f32)
            for c in range(chunks):
                state = got[b, c].astype(bf16)
                reading = dot(q_ref[...], state, 1, 0) * scale
                att[:, cols[c]] = att[:, cols[c]] + reading * lams[b, :, cols[c]].astype(f32)
                total = total + dot(wts[b, :, cols[c]], state, 1, 1)
            qg[...] = qg[...] + total * scale

    def share(which, j):
        return pltpu.make_async_remote_copy(
            src_ref=qk_send.at[which, peers[j]], dst_ref=qk_recv.at[which, j],
            send_sem=h_send.at[which, j], recv_sem=h_recv.at[which, j],
            device_id=(seq, peers[j]), device_id_type=MESH)

    def send_share(which, grad):
        for i in range(n_head):
            qk_send[which, i] = grad[i * rows:(i + 1) * rows]
        for j in range(n_head - 1):
            share(which, j).start()

    def step_forward(stage, c):
        if stage < low_bits:
            b = stage

            @pl.when(up_gets[b])
            def _():
                forward(b, c).wait_recv()
                own[b + 1, c] = own[b, c] + got[b, c]

            if b + 1 < low_bits:
                @pl.when(up_sends[b + 1])
                def _():
                    forward(b + 1, c).start()
            else:
                @pl.when(bit[mid] == 0)
                def _():
                    forward(mid, c).start()
        elif stage == low_bits:
            @pl.when(bit[mid] == 1)
            def _():
                forward(mid, c).wait_recv()

            @pl.when(line == 1)
            def _():
                own[top, c] = own[mid, c] + got[mid, c]
                forward(top, c).start()
        elif stage == low_bits + 1:
            @pl.when(line == 2)
            def _():
                forward(top, c).wait_recv()
                forward(top, c, True).start()
        else:
            @pl.when(line == 3)
            def _():
                forward(top, c).wait_recv()

    def pass_down(b, c):
        pend[b, c] = pend[b, c] + racc[c]

        @pl.when(down_sends[b])
        def _():
            backward(b, c).start()

    def step_backward(stage, c):
        if stage == 0:
            @pl.when(line == 2)
            def _():
                backward(top, c).wait_recv()
                pend[top, c] = pend[top, c] + back[top, c]
                backward(top, c).start()

            @pl.when(line == 3)
            def _():
                racc[c] = jnp.zeros((depth, LANES), f32)
                pass_down(low_bits - 1, c)
        elif stage == 1:
            @pl.when(line == 1)
            def _():
                backward(top, c).wait_recv()
                pend[mid, c] = pend[mid, c] + back[top, c]
                backward(mid, c).start()
                racc[c] = back[top, c]
                pass_down(low_bits - 1, c)

            @pl.when(line == 2)
            def _():
                backward(mid, c).wait_recv()
                racc[c] = back[mid, c]
                pass_down(low_bits - 1, c)
        elif stage == 2:
            @pl.when(line == 0)
            def _():
                backward(mid, c).wait_recv()
                racc[c] = back[mid, c]
                pass_down(low_bits - 1, c)
        else:
            b = low_bits - 1 - (stage - 3)

            @pl.when(down_gets[b])
            def _():
                backward(b, c).wait_recv()
                racc[c] = racc[c] + back[b, c]

            if b > 0:
                pass_down(b - 1, c)

    near_sum = None
    stages = low_bits + 3
    for c in range(chunks):
        unit(0, c)
    finish_block(0)
    for c in range(chunks):
        step_backward(0, c)
        step_forward(0, c)
    for stage in range(1, low_bits):
        for c in range(chunks):
            step_forward(stage, c)
    for c in range(chunks):
        step_backward(1, c)
        step_forward(low_bits, c)
    for c in range(chunks):
        step_backward(2, c)
        step_forward(low_bits + 1, c)
    for c in range(chunks):
        unit(1, c)
    finish_block(1)
    near_sum = near_level()
    for b in range(low_bits):
        consume(b)
    consume(mid)
    for c in range(chunks):
        step_forward(low_bits + 2, c)
    consume(top)
    send_share(0, qg[...])
    part = tokens // PIECES
    for p in range(PIECES):
        att_outs[p][...] = att[p * part:(p + 1) * part, :].astype(bf16)
    for stage in range(3, stages):
        for c in range(chunks):
            step_backward(stage, c)

    grad_low = kg[first_half, :]
    grad_high = kg[second_half, :]
    for c in range(chunks):
        incoming = racc[c]
        low = (incoming + near_sum[:, cols[c]]).astype(bf16)
        high = incoming.astype(bf16)
        grad_low = grad_low + dot(v_ref[first_half, cols[c]], low, 1, 1)
        grad_high = grad_high + dot(v_ref[second_half, cols[c]], high, 1, 1)
    send_share(1, jnp.concatenate([grad_low, grad_high], axis=0))
    for c in range(chunks):
        incoming = racc[c]
        low = (incoming + near_sum[:, cols[c]]).astype(bf16)
        high = incoming.astype(bf16)
        for half, state in ((first_half, low), (second_half, high)):
            final = (vg[half, cols[c]] + dot(k_ref[half, :], state, 1, 0)).astype(bf16)
            for p in range(PIECES // 2):
                vg_outs[half.start // part + p][:, cols[c]] = final[p * part:(p + 1) * part]

    for which, out in ((0, qg_out), (1, kg_out)):
        total = qk_send[which, head]
        for j in range(n_head - 1):
            share(which, j).wait_recv()
            total = total + qk_recv[which, j]
        out[...] = total
    for which in range(2):
        for j in range(n_head - 1):
            share(which, j).wait_send()
    for c in range(chunks):
        for b in range(low_bits):
            @pl.when(up_sends[b])
            def _(b=b, c=c):
                forward(b, c).wait_send()

            @pl.when(down_sends[b])
            def _(b=b, c=c):
                backward(b, c).wait_send()

        @pl.when(bit[mid] == 0)
        def _(c=c):
            forward(mid, c).wait_send()

        @pl.when(bit[mid] == 1)
        def _(c=c):
            backward(mid, c).wait_send()

        @pl.when(line == 1)
        def _(c=c):
            forward(top, c).wait_send()

        @pl.when(line == 2)
        def _(c=c):
            forward(top, c, True).wait_send()

        @pl.when(line >= 2)
        def _(c=c):
            backward(top, c).wait_send()


def per_device(n_seq, n_head, queries, keys, values, level_codes, cotangent):
    tokens, depth = queries.shape
    total_width = values.shape[1]
    chunks = total_width // LANES
    rows = tokens // n_head
    bits = n_seq.bit_length() - 1
    f32, bf16 = jnp.float32, jnp.bfloat16
    vmem = pl.BlockSpec(memory_space=pltpu.VMEM)
    links = (bits, chunks, depth, LANES)
    dma = pltpu.SemaphoreType.DMA
    results = pl.pallas_call(
        functools.partial(kernel, n_seq, n_head),
        out_shape=(
            *[jax.ShapeDtypeStruct((tokens // PIECES, total_width), bf16)] * (2 * PIECES),
            jax.ShapeDtypeStruct((rows, depth), f32),
            jax.ShapeDtypeStruct((rows, depth), f32),
        ),
        in_specs=[pl.BlockSpec(memory_space=pltpu.HBM)] * 5,
        out_specs=(vmem,) * (2 * PIECES + 2),
        scratch_shapes=[
            pltpu.VMEM((tokens, total_width), f32),
            pltpu.VMEM((tokens, total_width), f32),
            pltpu.VMEM((tokens, depth), f32),
            pltpu.VMEM((tokens, depth), f32),
            pltpu.VMEM((bits, tokens, total_width), bf16),
            pltpu.VMEM((bits, tokens, total_width), bf16),
            pltpu.VMEM(links, f32),
            pltpu.VMEM(links, f32),
            pltpu.VMEM(links, f32),
            pltpu.VMEM(links, f32),
            pltpu.VMEM((chunks, depth, LANES), f32),
            pltpu.VMEM((2, n_head, rows, depth), f32),
            pltpu.VMEM((2, n_head - 1, rows, depth), f32),
            dma((bits, chunks)),
            dma((bits, chunks)),
            dma((bits, chunks)),
            dma((bits, chunks)),
            dma((2, n_head - 1)),
            dma((2, n_head - 1)),
            pltpu.VMEM((tokens, depth), bf16),
            pltpu.VMEM((tokens, depth), bf16),
            pltpu.VMEM((tokens, total_width), bf16),
            pltpu.VMEM((level_codes.shape[1], level_codes.shape[0], tokens), jnp.int32),
            pltpu.VMEM((tokens, total_width), bf16),
            dma((5,)),
        ],
        compiler_params=pltpu.CompilerParams(
            collective_id=0, has_side_effects=True, vmem_limit_bytes=54656 * 1024),
    )(queries, keys, values, jnp.transpose(level_codes, (1, 0, 2)), cotangent)
    return hand_over(tokens, total_width, results)


def settle(*refs):
    att_parts, vg_parts = refs[:PIECES], refs[PIECES:2 * PIECES]
    qg, kg, att_out, qg_out, kg_out, vg_out, sems = refs[2 * PIECES:]
    part = att_parts[0].shape[0]
    pairs = [(qg, qg_out), (kg, kg_out)]
    for p in range(PIECES):
        pairs.append((att_parts[p], att_out.at[pl.ds(p * part, part)]))
        pairs.append((vg_parts[p], vg_out.at[pl.ds(p * part, part)]))
    copies = [pltpu.make_async_copy(a, b, sems.at[i]) for i, (a, b) in enumerate(pairs)]
    for one in copies:
        one.start()
    for one in copies:
        one.wait()


def hand_over(tokens, total_width, results):
    wide = jax.ShapeDtypeStruct((tokens, total_width), jnp.bfloat16)
    thin = jax.ShapeDtypeStruct(results[-1].shape, jnp.float32)
    anywhere = pl.BlockSpec(memory_space=pl.ANY)
    return pl.pallas_call(
        settle,
        out_shape=(wide, thin, thin, wide),
        in_specs=[anywhere] * len(results),
        out_specs=(anywhere,) * 4,
        scratch_shapes=[pltpu.SemaphoreType.DMA((len(results),))],
        compiler_params=pltpu.CompilerParams(vmem_limit_bytes=1024 * 1024),
    )(*results)


def solution(mesh):
    placed = (
        P("seq", None),
        P("seq", None),
        P("seq", "head"),
        P("head", None, "seq"),
        P("seq", "head"),
    )
    return jax.shard_map(
        functools.partial(per_device, mesh.shape["seq"], mesh.shape["head"]),
        mesh=mesh,
        in_specs=placed,
        out_specs=(
            P("seq", "head"),
            P(("seq", "head"), None),
            P(("seq", "head"), None),
            P("seq", "head"),
        ),
        check_vma=False,
    )
```

```python
import functools

import jax
import jax.numpy as jnp
from jax import lax
from jax.experimental import pallas as pl
from jax.experimental.pallas import tpu as pltpu
from jax.sharding import PartitionSpec as P

STRETCH_BITS = 7
STRETCH = 128
LANES = 128
SCALE_CODE = 0.125
MESH = pl.DeviceIdType.MESH
PIECES = 8
ROOM = 54656 * 1024


def dot(a, b, da, db):
    return lax.dot_general(a, b, (((da,), (db,)), ((), ())), preferred_element_type=jnp.float32)


def kernel(
    n_seq, n_head,
    q_in, k_in, v_in, code_in, g_in,
    *rest,
):
    att_outs, vg_outs = rest[:PIECES], rest[PIECES:2 * PIECES]
    (
    qg_out, kg_out,
    att, vg, qg, kg, wts, lams, own, got, pend, back, racc, qk_send, qk_recv,
    f_send, f_recv, b_send, b_recv, h_send, h_recv,
    q_ref, k_ref, v_ref, code_ref, g_ref, load) = rest[2 * PIECES:]
    loads = [
        pltpu.make_async_copy(src, dst, load.at[i])
        for i, (src, dst) in enumerate((
            (k_in, k_ref), (v_in, v_ref), (g_in, g_ref), (q_in, q_ref), (code_in, code_ref)))
    ]
    for one in loads:
        one.start()
    tokens, depth = q_ref.shape
    total_width = v_ref.shape[1]
    heads = code_ref.shape[1]
    width = total_width // heads
    chunks = total_width // LANES
    per_chunk = LANES // width
    blocks = tokens // STRETCH
    rows = tokens // n_head
    bits = n_seq.bit_length() - 1
    scale = depth ** -0.5
    near = STRETCH_BITS + 1
    far = near + 1
    f32, bf16 = jnp.float32, jnp.bfloat16
    seq, head = lax.axis_index("seq"), lax.axis_index("head")
    bit = [lax.rem(lax.div(seq, 1 << b), 2) for b in range(bits)]
    low_bits = bits - 2
    top, mid = bits - 1, bits - 2
    stride = 1 << mid
    line = lax.div(seq, stride)
    partner = [seq + (1 << b) * (1 - 2 * bit[b]) for b in range(low_bits)]
    peers = [lax.rem(head + j, n_head) for j in range(1, n_head)]

    barrier = pltpu.get_barrier_semaphore()

    def greet(to):
        pl.semaphore_signal(barrier, inc=1, device_id=to, device_id_type=MESH)

    for b in range(low_bits):
        greet((partner[b], head))
    for peer in peers:
        greet((seq, peer))

    @pl.when(line > 0)
    def _():
        greet((seq - stride, head))

    @pl.when(line < 3)
    def _():
        greet((seq + stride, head))

    greetings = low_bits + n_head - 1 + (line > 0).astype(jnp.int32) + (line < 3).astype(jnp.int32)

    def forward(b, c, relay=False):
        return pltpu.make_async_remote_copy(
            src_ref=(got if relay else own).at[b, c], dst_ref=got.at[b, c],
            send_sem=f_send.at[b, c], recv_sem=f_recv.at[b, c],
            device_id=(partner[b] if b < low_bits else seq + stride, head), device_id_type=MESH)

    def backward(b, c):
        return pltpu.make_async_remote_copy(
            src_ref=pend.at[b, c], dst_ref=back.at[b, c],
            send_sem=b_send.at[b, c], recv_sem=b_recv.at[b, c],
            device_id=(partner[b] if b < low_bits else seq - stride, head), device_id_type=MESH)

    highest = [lax.div(seq, 2 << b) == (n_seq >> (b + 1)) - 1 for b in range(low_bits)]
    up_sends = [jnp.logical_or(bit[b] == 0, jnp.logical_not(highest[b])) for b in range(low_bits)]
    up_gets = [jnp.logical_or(bit[b] == 1, jnp.logical_not(highest[b])) for b in range(low_bits)]
    down_sends, down_gets = up_gets, up_sends

    cols = [slice(c * LANES, (c + 1) * LANES) for c in range(chunks)]

    spread = (
        lax.broadcasted_iota(jnp.int32, (heads, total_width), 1) // width
        == lax.broadcasted_iota(jnp.int32, (heads, total_width), 0)
    ).astype(f32)

    def level_weights(level):
        lam = code_ref[level].astype(f32) * SCALE_CODE
        return dot(lam, spread, 0, 0)

    def prepare(b):
        @pl.when(bit[b] == 1)
        def _():
            lam = level_weights(far + b)
            lams[b] = lam.astype(bf16)
            weighted = (g_ref[...].astype(f32) * lam).astype(bf16)
            wts[b] = weighted
            sending = dot(q_ref[...], weighted, 0, 0) * scale
            for c in range(chunks):
                pend[b, c] = sending[:, cols[c]]

        if b < low_bits:
            @pl.when(bit[b] == 0)
            def _():
                for c in range(chunks):
                    pend[b, c] = jnp.zeros((depth, LANES), f32)

    first_half = slice(0, STRETCH)
    second_half = slice(STRETCH, 2 * STRETCH)
    loads[0].wait()
    loads[1].wait()
    state_low = dot(k_ref[first_half, :], v_ref[first_half, :], 0, 0)
    state_all = state_low + dot(k_ref[second_half, :], v_ref[second_half, :], 0, 0)
    for c in range(chunks):
        own[0, c] = state_all[:, cols[c]]
    pl.semaphore_wait(barrier, greetings)
    for c in range(chunks):
        @pl.when(up_sends[0])
        def _(c=c):
            forward(0, c).start()
    for one in loads[2:]:
        one.wait()
    prepare(top)
    for c in range(chunks):
        @pl.when(line == 3)
        def _(c=c):
            backward(top, c).start()
    prepare(mid)
    for c in range(chunks):
        @pl.when(line == 3)
        def _(c=c):
            backward(mid, c).start()
    for b in range(low_bits - 1, -1, -1):
        prepare(b)

    key_pos = lax.rem(lax.broadcasted_iota(jnp.int32, (per_chunk * STRETCH, STRETCH), 0), STRETCH)
    query_pos = lax.broadcasted_iota(jnp.int32, (per_chunk * STRETCH, STRETCH), 1)
    differ = jnp.bitwise_xor(query_pos, key_pos)
    causal = key_pos <= query_pos
    lane_head = lax.broadcasted_iota(jnp.int32, (STRETCH, LANES), 1) // width

    def split_heads(block):
        block = block.astype(f32)
        return jnp.concatenate(
            [jnp.where(lane_head == i, block, 0.0) for i in range(per_chunk)], axis=0).astype(bf16)

    press_sum = [jnp.zeros((STRETCH, STRETCH), f32) for _ in range(blocks)]
    scores = []
    for n in range(blocks):
        at = slice(n * STRETCH, (n + 1) * STRETCH)
        one = dot(k_ref[at, :], q_ref[at, :], 1, 1) * scale
        scores.append(jnp.concatenate([one] * per_chunk, axis=0))

    def unit(n, c):
        at = slice(n * STRETCH, (n + 1) * STRETCH)

        def rows_of(level):
            parts = []
            for i in range(per_chunk):
                row = code_ref[level, c * per_chunk + i:c * per_chunk + i + 1, at].astype(f32) * SCALE_CODE
                parts.append(jnp.broadcast_to(row, (STRETCH, STRETCH)))
            return jnp.concatenate(parts, axis=0)

        mask = rows_of(STRETCH_BITS)
        for level in range(STRETCH_BITS - 1, -1, -1):
            mask = jnp.where(differ < (1 << level), rows_of(level), mask)
        mask = jnp.where(causal, mask, 0.0)
        mixed = (scores[n] * mask).astype(bf16)
        v_split = split_heads(v_ref[at, cols[c]])
        g_block = g_ref[at, cols[c]]
        att[at, cols[c]] = dot(mixed, v_split, 0, 0)
        wide = jnp.concatenate(
            [mixed[i * STRETCH:(i + 1) * STRETCH] for i in range(per_chunk)], axis=1)
        vg[at, cols[c]] = dot(wide, split_heads(g_block), 1, 0)
        press = dot(v_split, g_block, 1, 1) * mask
        for i in range(per_chunk):
            press_sum[n] = press_sum[n] + press[i * STRETCH:(i + 1) * STRETCH]

    def finish_block(n):
        at = slice(n * STRETCH, (n + 1) * STRETCH)
        press = press_sum[n].astype(bf16)
        qg[at, :] = dot(press, k_ref[at, :], 0, 0) * scale
        kg[at, :] = dot(press, q_ref[at, :], 1, 0) * scale

    def near_level():
        low = state_low.astype(bf16)
        lam = level_weights(near)[second_half]
        att[second_half, :] = att[second_half, :] + lam * (
            dot(q_ref[second_half, :], low, 1, 0) * scale)
        weighted = (g_ref[second_half, :].astype(f32) * lam).astype(bf16)
        qg[second_half, :] = qg[second_half, :] + dot(weighted, low, 1, 1) * scale
        return dot(q_ref[second_half, :], weighted, 0, 0) * scale

    def consume(b):
        @pl.when(bit[b] == 1)
        def _():
            total = jnp.zeros((tokens, depth), f32)
            for c in range(chunks):
                state = got[b, c].astype(bf16)
                reading = dot(q_ref[...], state, 1, 0) * scale
                att[:, cols[c]] = att[:, cols[c]] + reading * lams[b, :, cols[c]].astype(f32)
                total = total + dot(wts[b, :, cols[c]], state, 1, 1)
            qg[...] = qg[...] + total * scale

    def share(which, j):
        return pltpu.make_async_remote_copy(
            src_ref=qk_send.at[which, peers[j]], dst_ref=qk_recv.at[which, j],
            send_sem=h_send.at[which, j], recv_sem=h_recv.at[which, j],
            device_id=(seq, peers[j]), device_id_type=MESH)

    def send_share(which, grad):
        for i in range(n_head):
            qk_send[which, i] = grad[i * rows:(i + 1) * rows]
        for j in range(n_head - 1):
            share(which, j).start()

    def step_forward(stage, c):
        if stage < low_bits:
            b = stage

            @pl.when(up_gets[b])
            def _():
                forward(b, c).wait_recv()
                own[b + 1, c] = own[b, c] + got[b, c]

            if b + 1 < low_bits:
                @pl.when(up_sends[b + 1])
                def _():
                    forward(b + 1, c).start()
            else:
                @pl.when(bit[mid] == 0)
                def _():
                    forward(mid, c).start()
        elif stage == low_bits:
            @pl.when(bit[mid] == 1)
            def _():
                forward(mid, c).wait_recv()

            @pl.when(line == 1)
            def _():
                own[top, c] = own[mid, c] + got[mid, c]
                forward(top, c).start()
        elif stage == low_bits + 1:
            @pl.when(line == 2)
            def _():
                forward(top, c).wait_recv()
                forward(top, c, True).start()
        else:
            @pl.when(line == 3)
            def _():
                forward(top, c).wait_recv()

    def pass_down(b, c):
        pend[b, c] = pend[b, c] + racc[c]

        @pl.when(down_sends[b])
        def _():
            backward(b, c).start()

    def step_backward(stage, c):
        if stage == 0:
            @pl.when(line == 2)
            def _():
                backward(top, c).wait_recv()
                pend[top, c] = pend[top, c] + back[top, c]
                backward(top, c).start()

            @pl.when(line == 3)
            def _():
                racc[c] = jnp.zeros((depth, LANES), f32)
                pass_down(low_bits - 1, c)
        elif stage == 1:
            @pl.when(line == 1)
            def _():
                backward(top, c).wait_recv()
                pend[mid, c] = pend[mid, c] + back[top, c]
                backward(mid, c).start()
                racc[c] = back[top, c]
                pass_down(low_bits - 1, c)

            @pl.when(line == 2)
            def _():
                backward(mid, c).wait_recv()
                racc[c] = back[mid, c]
                pass_down(low_bits - 1, c)
        elif stage == 2:
            @pl.when(line == 0)
            def _():
                backward(mid, c).wait_recv()
                racc[c] = back[mid, c]
                pass_down(low_bits - 1, c)
        else:
            b = low_bits - 1 - (stage - 3)

            @pl.when(down_gets[b])
            def _():
                backward(b, c).wait_recv()
                racc[c] = racc[c] + back[b, c]

            if b > 0:
                pass_down(b - 1, c)

    near_sum = None
    stages = low_bits + 3
    for c in range(chunks):
        unit(0, c)
    finish_block(0)
    for c in range(chunks):
        step_backward(0, c)
        step_forward(0, c)
    for stage in range(1, low_bits):
        for c in range(chunks):
            step_forward(stage, c)
    for c in range(chunks):
        step_backward(1, c)
        step_forward(low_bits, c)
    for c in range(chunks):
        step_backward(2, c)
        step_forward(low_bits + 1, c)
    for c in range(chunks):
        unit(1, c)
    finish_block(1)
    near_sum = near_level()
    for b in range(low_bits):
        consume(b)
    consume(mid)
    for c in range(chunks):
        step_forward(low_bits + 2, c)
    consume(top)
    send_share(0, qg[...])
    part = tokens // PIECES
    for p in range(PIECES):
        att_outs[p][...] = att[p * part:(p + 1) * part, :].astype(bf16)
    for stage in range(3, stages):
        for c in range(chunks):
            step_backward(stage, c)

    grad_low = kg[first_half, :]
    grad_high = kg[second_half, :]
    for c in range(chunks):
        incoming = racc[c]
        low = (incoming + near_sum[:, cols[c]]).astype(bf16)
        high = incoming.astype(bf16)
        grad_low = grad_low + dot(v_ref[first_half, cols[c]], low, 1, 1)
        grad_high = grad_high + dot(v_ref[second_half, cols[c]], high, 1, 1)
    send_share(1, jnp.concatenate([grad_low, grad_high], axis=0))
    for c in range(chunks):
        incoming = racc[c]
        low = (incoming + near_sum[:, cols[c]]).astype(bf16)
        high = incoming.astype(bf16)
        for half, state in ((first_half, low), (second_half, high)):
            final = (vg[half, cols[c]] + dot(k_ref[half, :], state, 1, 0)).astype(bf16)
            for p in range(PIECES // 2):
                vg_outs[half.start // part + p][:, cols[c]] = final[p * part:(p + 1) * part]

    for which, out in ((0, qg_out), (1, kg_out)):
        total = qk_send[which, head]
        for j in range(n_head - 1):
            share(which, j).wait_recv()
            total = total + qk_recv[which, j]
        out[...] = total
    for which in range(2):
        for j in range(n_head - 1):
            share(which, j).wait_send()
    for c in range(chunks):
        for b in range(low_bits):
            @pl.when(up_sends[b])
            def _(b=b, c=c):
                forward(b, c).wait_send()

            @pl.when(down_sends[b])
            def _(b=b, c=c):
                backward(b, c).wait_send()

        @pl.when(bit[mid] == 0)
        def _(c=c):
            forward(mid, c).wait_send()

        @pl.when(bit[mid] == 1)
        def _(c=c):
            backward(mid, c).wait_send()

        @pl.when(line == 1)
        def _(c=c):
            forward(top, c).wait_send()

        @pl.when(line == 2)
        def _(c=c):
            forward(top, c, True).wait_send()

        @pl.when(line >= 2)
        def _(c=c):
            backward(top, c).wait_send()


def on_any(n_seq, n_head, queries, keys, values, level_codes, cotangent):
    tokens, depth = queries.shape
    total_width = values.shape[1]
    chunks = total_width // LANES
    rows = tokens // n_head
    bits = n_seq.bit_length() - 1
    f32, bf16 = jnp.float32, jnp.bfloat16
    vmem = pl.BlockSpec(memory_space=pltpu.VMEM)
    links = (bits, chunks, depth, LANES)
    dma = pltpu.SemaphoreType.DMA
    results = pl.pallas_call(
        functools.partial(kernel, n_seq, n_head),
        out_shape=(
            *[jax.ShapeDtypeStruct((tokens // PIECES, total_width), bf16)] * (2 * PIECES),
            jax.ShapeDtypeStruct((rows, depth), f32),
            jax.ShapeDtypeStruct((rows, depth), f32),
        ),
        in_specs=[pl.BlockSpec(memory_space=pltpu.HBM)] * 5,
        out_specs=(vmem,) * (2 * PIECES + 2),
        scratch_shapes=[
            pltpu.VMEM((tokens, total_width), f32),
            pltpu.VMEM((tokens, total_width), f32),
            pltpu.VMEM((tokens, depth), f32),
            pltpu.VMEM((tokens, depth), f32),
            pltpu.VMEM((bits, tokens, total_width), bf16),
            pltpu.VMEM((bits, tokens, total_width), bf16),
            pltpu.VMEM(links, f32),
            pltpu.VMEM(links, f32),
            pltpu.VMEM(links, f32),
            pltpu.VMEM(links, f32),
            pltpu.VMEM((chunks, depth, LANES), f32),
            pltpu.VMEM((2, n_head, rows, depth), f32),
            pltpu.VMEM((2, n_head - 1, rows, depth), f32),
            dma((bits, chunks)),
            dma((bits, chunks)),
            dma((bits, chunks)),
            dma((bits, chunks)),
            dma((2, n_head - 1)),
            dma((2, n_head - 1)),
            pltpu.VMEM((tokens, depth), bf16),
            pltpu.VMEM((tokens, depth), bf16),
            pltpu.VMEM((tokens, total_width), bf16),
            pltpu.VMEM((level_codes.shape[1], level_codes.shape[0], tokens), jnp.int32),
            pltpu.VMEM((tokens, total_width), bf16),
            dma((5,)),
        ],
        compiler_params=pltpu.CompilerParams(
            collective_id=0, has_side_effects=True, vmem_limit_bytes=ROOM),
    )(queries, keys, values, jnp.transpose(level_codes, (1, 0, 2)), cotangent)
    return hand_over(tokens, total_width, results)


def settle(*refs):
    att_parts, vg_parts = refs[:PIECES], refs[PIECES:2 * PIECES]
    qg, kg, att_out, qg_out, kg_out, vg_out, sems = refs[2 * PIECES:]
    part = att_parts[0].shape[0]
    pairs = [(qg, qg_out), (kg, kg_out)]
    for p in range(PIECES):
        pairs.append((att_parts[p], att_out.at[pl.ds(p * part, part)]))
        pairs.append((vg_parts[p], vg_out.at[pl.ds(p * part, part)]))
    copies = [pltpu.make_async_copy(a, b, sems.at[i]) for i, (a, b) in enumerate(pairs)]
    for one in copies:
        one.start()
    for one in copies:
        one.wait()


def hand_over(tokens, total_width, results):
    wide = jax.ShapeDtypeStruct((tokens, total_width), jnp.bfloat16)
    thin = jax.ShapeDtypeStruct(results[-1].shape, jnp.float32)
    anywhere = pl.BlockSpec(memory_space=pl.ANY)
    return pl.pallas_call(
        settle,
        out_shape=(wide, thin, thin, wide),
        in_specs=[anywhere] * len(results),
        out_specs=(anywhere,) * 4,
        scratch_shapes=[pltpu.SemaphoreType.DMA((len(results),))],
        compiler_params=pltpu.CompilerParams(vmem_limit_bytes=1024 * 1024),
    )(*results)


SUBS = 2
AHEAD = (3, 2, 1)


def line_kernel(n_head, names, q_in, k_in, v_in, code_in, g_in, *rest):
    att_outs, vg_outs = rest[:PIECES], rest[PIECES:2 * PIECES]
    qg_out, kg_out = rest[2 * PIECES:2 * PIECES + 2]
    r = dict(zip(names, rest[2 * PIECES + 2:]))
    att, vg, qg, kg, wts, lams = (r[n] for n in ("att", "vg", "qg", "kg", "wts", "lams"))
    own, sx, rr, gm, tt, gt = (r[n] for n in ("own", "sx", "rr", "gm", "tt", "gt"))
    w0, wmid, wtop, rz, zz, gz = (r[n] for n in ("w0", "wmid", "wtop", "rz", "zz", "gz"))
    ux, us, gu, g0, hb, hs, hx = (r[n] for n in ("ux", "us", "gu", "g0", "hb", "hs", "hx"))
    nearby, qk_send, qk_recv = (r[n] for n in ("nearby", "qk_send", "qk_recv"))
    q_ref, k_ref, v_ref, code_ref, g_ref = (r[n] for n in ("q", "k", "v", "code", "g"))
    load, entry = r["load"], r["entry"]

    loads = [
        pltpu.make_async_copy(src, dst, load.at[i])
        for i, (src, dst) in enumerate((
            (k_in, k_ref), (v_in, v_ref), (g_in, g_ref), (q_in, q_ref), (code_in, code_ref)))
    ]
    for one in loads:
        one.start()
    tokens, depth = q_ref.shape
    total_width = v_ref.shape[1]
    heads = code_ref.shape[1]
    width = total_width // heads
    chunks = total_width // LANES
    per_chunk = LANES // width
    blocks = tokens // STRETCH
    share_rows = tokens // n_head
    scale = depth ** -0.5
    near = STRETCH_BITS + 1
    far = near + 1
    top, mid = 2, 1
    half_width = total_width // 2
    f32, bf16 = jnp.float32, jnp.bfloat16
    seq, head = lax.axis_index("seq"), lax.axis_index("head")
    x = lax.rem(seq, 2)
    line = lax.div(seq, 2)
    low = lax.rem(line, 2)
    across = seq + 1 - 2 * x
    peers = [lax.rem(head + j, n_head) for j in range(1, n_head)]

    def when(*conditions):
        return pl.when(functools.reduce(jnp.logical_and, conditions))

    left, right = x == 0, x == 1
    early, late = line < 2, line >= 2
    even, odd = low == 0, low == 1
    barrier = pltpu.get_barrier_semaphore()

    def greet(to, sem=barrier):
        pl.semaphore_signal(sem, inc=1, device_id=to, device_id_type=MESH)

    greet((across, head))
    for peer in peers:
        greet((seq, peer))

    @when(line == 0)
    def _():
        greet((seq + 2, head))

    @when(early)
    def _():
        greet((x + 4, head))
        greet((x + 6, head))

    @when(late)
    def _():
        greet((seq + 2 - 4 * low, head))
        greet((across + 2 - 4 * low, head))

    def rows(s):
        return pl.ds(s * (depth // SUBS), depth // SUBS)

    subs = [(j, s) for j in range(2) for s in range(SUBS)]

    def mine(j):
        return 2 * x + j

    def other(j):
        return 2 * (1 - x) + j

    def remote(src, dst, send, recv, to):
        return pltpu.make_async_remote_copy(
            src_ref=src, dst_ref=dst, send_sem=send, recv_sem=recv,
            device_id=(to, head), device_id_type=MESH)

    def f1(c, s):
        return remote(own.at[c, rows(s)], sx.at[c, rows(s)],
                      r["f1s"].at[c, s], r["f1r"].at[c, s], across)

    def f2(j, s):
        return remote(rr.at[j, rows(s)], gm.at[mine(j), rows(s)],
                      r["f2s"].at[j, s], r["f2r"].at[j, s], seq + 2)

    def agm(c, j, s):
        return remote(gm.at[c, rows(s)], gm.at[c, rows(s)],
                      r["agms"].at[j, s], r["agmr"].at[j, s], across)

    def f3(d, j, s):
        return remote(tt.at[j, rows(s)], gt.at[mine(j), rows(s)],
                      r["f3s"].at[d, j, s], r["f3r"].at[j, s], seq + 4 - 2 * d)

    def agt(c, j, s):
        return remote(gt.at[c, rows(s)], gt.at[c, rows(s)],
                      r["agts"].at[j, s], r["agtr"].at[j, s], across)

    def b1(i, s):
        there_x = x if i % 2 == 0 else 1 - x
        there_low = low if i < 2 else 1 - low
        to = seq + (there_x - x) + 2 * (there_low - low)
        return remote(wtop.at[2 * there_x + there_low, rows(s)], rz.at[i - 1, rows(s)],
                      r["b1s"].at[i - 1, s], r["b1r"].at[i - 1, s], to)

    def b2(d, j, s):
        return remote(zz.at[rows(s)], gz.at[j, rows(s)],
                      r["b2s"].at[d, s], r["b2r"].at[j, s], x + 2 * d)

    def u1(c, j):
        return remote(wmid.at[c], ux.at[j], r["u1s"].at[j], r["u1r"].at[j], across)

    def u2(j):
        return remote(us.at[j], gu.at[j], r["u2s"].at[j], r["u2r"].at[j], seq - 2)

    def w0a(j):
        return remote(w0.at[j], g0.at[j], r["w0s"].at[j], r["w0r"].at[j], across)

    def agb(j, s):
        return remote(hs.at[j, rows(s)], hx.at[j, rows(s)],
                      r["agbs"].at[j, s], r["agbr"].at[j, s], across)

    def share(which, j):
        return pltpu.make_async_remote_copy(
            src_ref=qk_send.at[which, peers[j]], dst_ref=qk_recv.at[which, j],
            send_sem=r["hs_"].at[which, j], recv_sem=r["hr_"].at[which, j],
            device_id=(seq, peers[j]), device_id_type=MESH)

    def send_share(which, grad):
        for i in range(n_head):
            qk_send[which, i] = grad[i * share_rows:(i + 1) * share_rows]
        for j in (1, 2, 0) if n_head == 4 else range(n_head - 1):
            share(which, j).start()

    cols = [slice(c * LANES, (c + 1) * LANES) for c in range(chunks)]
    spread = (
        lax.broadcasted_iota(jnp.int32, (heads, total_width), 1) // width
        == lax.broadcasted_iota(jnp.int32, (heads, total_width), 0)
    ).astype(f32)

    def level_weights(level):
        lam = code_ref[level].astype(f32) * SCALE_CODE
        return dot(lam, spread, 0, 0)

    def prepare(b, into):
        lam = level_weights(far + b)
        lams[b] = lam.astype(bf16)
        weighted = (g_ref[...].astype(f32) * lam).astype(bf16)
        wts[b] = weighted
        sending = dot(q_ref[...], weighted, 0, 0) * scale
        for c in range(chunks):
            into[c] = sending[:, cols[c]]

    first_half = slice(0, STRETCH)
    second_half = slice(STRETCH, 2 * STRETCH)
    for one in loads:
        one.wait()

    @when(late)
    def _():
        prepare(top, wtop)
        pl.semaphore_wait(barrier, n_head + 4)
        for s in range(SUBS):
            for i in AHEAD:
                b1(i, s).start()
        greet((x + 2, head), entry)

    state_low = dot(k_ref[first_half, :], v_ref[first_half, :], 0, 0)
    state_all = state_low + dot(k_ref[second_half, :], v_ref[second_half, :], 0, 0)
    for c in range(chunks):
        own[c] = state_all[:, cols[c]]

    @when(line == 0)
    def _():
        pl.semaphore_wait(barrier, n_head)

    @when(line == 1)
    def _():
        pl.semaphore_wait(barrier, n_head + 1)
        greet((x, head), entry)

    @when(line < 3)
    def _():
        for j, s in subs:
            f1(other(j), s).start()

    @when(odd)
    def _():
        prepare(mid, wmid)
        for j in range(2):
            u1(other(j), j).start()

    @when(right)
    def _():
        prepare(0, w0)

    key_pos = lax.rem(lax.broadcasted_iota(jnp.int32, (per_chunk * STRETCH, STRETCH), 0), STRETCH)
    query_pos = lax.broadcasted_iota(jnp.int32, (per_chunk * STRETCH, STRETCH), 1)
    differ = jnp.bitwise_xor(query_pos, key_pos)
    causal = key_pos <= query_pos
    lane_head = lax.broadcasted_iota(jnp.int32, (STRETCH, LANES), 1) // width

    def split_heads(block):
        block = block.astype(f32)
        return jnp.concatenate(
            [jnp.where(lane_head == i, block, 0.0) for i in range(per_chunk)], axis=0).astype(bf16)

    def do_block(n):
        at = slice(n * STRETCH, (n + 1) * STRETCH)
        one = dot(k_ref[at, :], q_ref[at, :], 1, 1) * scale
        scores = jnp.concatenate([one] * per_chunk, axis=0)
        press_sum = jnp.zeros((STRETCH, STRETCH), f32)
        for c in range(chunks):
            def rows_of(level):
                parts = []
                for i in range(per_chunk):
                    row = code_ref[level, c * per_chunk + i:c * per_chunk + i + 1, at].astype(f32) * SCALE_CODE
                    parts.append(jnp.broadcast_to(row, (STRETCH, STRETCH)))
                return jnp.concatenate(parts, axis=0)

            mask = rows_of(STRETCH_BITS)
            for level in range(STRETCH_BITS - 1, -1, -1):
                mask = jnp.where(differ < (1 << level), rows_of(level), mask)
            mask = jnp.where(causal, mask, 0.0)
            mixed = (scores * mask).astype(bf16)
            v_split = split_heads(v_ref[at, cols[c]])
            g_block = g_ref[at, cols[c]]
            att[at, cols[c]] = dot(mixed, v_split, 0, 0)
            wide = jnp.concatenate(
                [mixed[i * STRETCH:(i + 1) * STRETCH] for i in range(per_chunk)], axis=1)
            vg[at, cols[c]] = dot(wide, split_heads(g_block), 1, 0)
            press = dot(v_split, g_block, 1, 1) * mask
            for i in range(per_chunk):
                press_sum = press_sum + press[i * STRETCH:(i + 1) * STRETCH]
        press_sum = press_sum.astype(bf16)
        qg[at, :] = dot(press_sum, k_ref[at, :], 0, 0) * scale
        kg[at, :] = dot(press_sum, q_ref[at, :], 1, 0) * scale

    def near_level():
        state = state_low.astype(bf16)
        lam = level_weights(near)[second_half]
        att[second_half, :] = att[second_half, :] + lam * (
            dot(q_ref[second_half, :], state, 1, 0) * scale)
        weighted = (g_ref[second_half, :].astype(f32) * lam).astype(bf16)
        qg[second_half, :] = qg[second_half, :] + dot(weighted, state, 1, 1) * scale
        nearby[...] = dot(q_ref[second_half, :], weighted, 0, 0) * scale

    def span(side):
        return pl.ds(pl.multiple_of(side * half_width, half_width), half_width)

    def read_state(b, side, ref):
        at = span(side)
        state = jnp.concatenate([ref[2 * side], ref[2 * side + 1]], axis=1).astype(bf16)
        reading = dot(q_ref[...], state, 1, 0) * scale
        total = att[:, at] + reading * lams[b, :, at].astype(f32)
        qg[...] = qg[...] + dot(wts[b, :, at], state, 1, 1) * scale
        return total

    def consume(b, side, ref):
        att[:, span(side)] = read_state(b, side, ref)

    part = tokens // PIECES

    def write_att(side, total):
        total = total.astype(bf16)
        for p in range(PIECES):
            att_outs[p][:, span(side)] = total[p * part:(p + 1) * part]

    def take_incoming(side, pair):
        at = span(side)
        incoming = jnp.concatenate(pair, axis=1)
        for half, state in (
                (first_half, incoming + nearby[:, at]), (second_half, incoming)):
            state = state.astype(bf16)
            kg[half, :] = kg[half, :] + dot(v_ref[half, at], state, 1, 1)
            final = (vg[half, at] + dot(k_ref[half, :], state, 1, 0)).astype(bf16)
            for p in range(PIECES // 2):
                vg_outs[half.start // part + p][:, at] = final[p * part:(p + 1) * part]

    do_block(0)

    @when(late)
    def _():
        for s in range(SUBS):
            for i in AHEAD:
                b1(i, s).wait_recv()
            zz[rows(s)] = (wtop[mine(low), rows(s)] + rz[0, rows(s)]) + (
                rz[1, rows(s)] + rz[2, rows(s)])
            b2(0, low, s).start()
        for s in range(SUBS):
            b2(1, low, s).start()

    @when(line == 0)
    def _():
        pl.semaphore_wait(entry, 1)

    @when(line < 3)
    def _():
        for j, s in subs:
            f1(mine(j), s).wait_recv()
            rr[j, rows(s)] = own[mine(j), rows(s)] + sx[mine(j), rows(s)]

            @when(even)
            def _():
                f2(j, s).start()

    @when(odd)
    def _():
        for j in range(2):
            u1(mine(j), j).wait_recv()
            us[j] = wmid[mine(j)] + ux[j]
            u2(j).start()

    @when(left)
    def _():
        for j, s in subs:
            f1(j, s).start()

    @when(left, line == 3)
    def _():
        for j, s in subs:
            f1(2 + j, s).start()

    @when(right)
    def _():
        for j in range(2):
            w0a(j).start()

    do_block(1)
    near_level()

    @when(line == 1)
    def _():
        pl.semaphore_wait(entry, 2)
        for j, s in subs:
            f2(j, s).wait_recv()
            tt[j, rows(s)] = gm[mine(j), rows(s)] + rr[j, rows(s)]
            f3(0, j, s).start()
            f3(1, j, s).start()
        for j, s in subs:
            agm(mine(j), j, s).start()

    def read_neighbour():
        @when(right, line < 3)
        def _():
            for j, s in subs:
                f1(j, s).wait_recv()

        @when(right, line == 3)
        def _():
            for c in range(chunks):
                for s in range(SUBS):
                    f1(c, s).wait_recv()

        @when(right)
        def _():
            consume(0, 0, sx)
            consume(0, 1, sx)

    def read_mid():
        consume(mid, x, gm)
        for j, s in subs:
            agm(other(j), j, s).wait_recv()
        consume(mid, 1 - x, gm)

    def pass_across(j, s, total):
        hb[j, rows(s)] = total

        @when(left)
        def _():
            hs[j, rows(s)] = total

        @when(right)
        def _():
            hs[j, rows(s)] = total + w0[2 + j, rows(s)]

        agb(j, s).start()

    def take_own():
        @when(left)
        def _():
            for j in range(2):
                w0a(j).wait_recv()
                hb[j] = hb[j] + g0[j]
        take_incoming(x, [hb[0], hb[1]])

    def take_other():
        for j, s in subs:
            agb(j, s).wait_recv()
        take_incoming(1 - x, [hx[0], hx[1]])

    @when(early)
    def _():
        read_neighbour()

        @when(line == 1)
        def _():
            read_mid()

        send_share(0, qg[...])
        write_att(0, att[:, :half_width])
        write_att(1, att[:, half_width:])

        @when(line == 0)
        def _():
            for j in range(2):
                u2(j).wait_recv()
        for j, s in subs:
            b2(0, j, s).wait_recv()

            @when(line == 0)
            def _():
                gz[j, rows(s)] = gz[j, rows(s)] + gu[j, rows(s)]
            pass_across(j, s, gz[j, rows(s)])
        take_own()
        take_other()
        send_share(1, kg[...])

    @when(late)
    def _():
        @when(line == 2)
        def _():
            for j in range(2):
                u2(j).wait_recv()
                for s in range(SUBS):
                    pass_across(j, s, gu[j, rows(s)])

        @when(line == 3)
        def _():
            for j, s in subs:
                hb[j, rows(s)] = jnp.zeros((depth // SUBS, LANES), f32)

            @when(right)
            def _():
                for j, s in subs:
                    hs[j, rows(s)] = w0[2 + j, rows(s)]
                    hx[j, rows(s)] = jnp.zeros((depth // SUBS, LANES), f32)
                    agb(j, s).start()
            for j, s in subs:
                f2(j, s).wait_recv()
                agm(mine(j), j, s).start()

        for j, s in subs:
            f3(0, j, s).wait_recv()
            agt(mine(j), j, s).start()
        read_neighbour()

        @when(line == 3)
        def _():
            read_mid()

        take_own()

        @when(jnp.logical_or(left, line == 2))
        def _():
            for j, s in subs:
                agb(j, s).wait_recv()
        take_incoming(1 - x, [hx[0], hx[1]])
        send_share(1, kg[...])
        write_att(x, read_state(top, x, gt))
        for j, s in subs:
            agt(other(j), j, s).wait_recv()
        total = read_state(top, 1 - x, gt)
        send_share(0, qg[...])
        write_att(1 - x, total)

    def collect(which, out):
        total = qk_send[which, head]
        for j in range(n_head - 1):
            share(which, j).wait_recv()
            total = total + qk_recv[which, j]
        out[...] = total

    collect(0, qg_out)
    collect(1, kg_out)

    for which in range(2):
        for j in range(n_head - 1):
            share(which, j).wait_send()

    @when(line < 3)
    def _():
        for j, s in subs:
            f1(other(j), s).wait_send()

    @when(left)
    def _():
        for j, s in subs:
            f1(j, s).wait_send()

    @when(left, line == 3)
    def _():
        for j, s in subs:
            f1(2 + j, s).wait_send()

    @when(even)
    def _():
        for j, s in subs:
            f2(j, s).wait_send()

    @when(odd)
    def _():
        for j, s in subs:
            agm(mine(j), j, s).wait_send()
        for j in range(2):
            u1(other(j), j).wait_send()
            u2(j).wait_send()

    @when(line == 1)
    def _():
        for j, s in subs:
            f3(0, j, s).wait_send()
            f3(1, j, s).wait_send()

    @when(late)
    def _():
        for j, s in subs:
            agt(mine(j), j, s).wait_send()
        for s in range(SUBS):
            for i in AHEAD:
                b1(i, s).wait_send()
            for d in range(2):
                b2(d, low, s).wait_send()

    @when(right)
    def _():
        for j in range(2):
            w0a(j).wait_send()

    @when(jnp.logical_or(right, line < 3))
    def _():
        for j, s in subs:
            agb(j, s).wait_send()


def line_scratch(tokens, depth, total_width, code_shape, n_head):
    chunks = total_width // LANES
    rows = tokens // n_head
    f32, bf16 = jnp.float32, jnp.bfloat16
    dma = pltpu.SemaphoreType.DMA

    def states(*lead):
        return pltpu.VMEM((*lead, depth, LANES), f32)

    return {
        "att": pltpu.VMEM((tokens, total_width), f32),
        "vg": pltpu.VMEM((tokens, total_width), f32),
        "qg": pltpu.VMEM((tokens, depth), f32),
        "kg": pltpu.VMEM((tokens, depth), f32),
        "wts": pltpu.VMEM((3, tokens, total_width), bf16),
        "lams": pltpu.VMEM((3, tokens, total_width), bf16),
        **{n: states(chunks) for n in ("own", "sx", "gm", "gt", "w0", "wmid", "wtop")},
        **{n: states(2) for n in ("rr", "tt", "gz", "ux", "us", "gu", "g0", "hb", "hs", "hx")},
        "rz": states(3),
        "zz": states(),
        "nearby": pltpu.VMEM((depth, total_width), f32),
        "qk_send": pltpu.VMEM((2, n_head, rows, depth), f32),
        "qk_recv": pltpu.VMEM((2, n_head - 1, rows, depth), f32),
        "q": pltpu.VMEM((tokens, depth), bf16),
        "k": pltpu.VMEM((tokens, depth), bf16),
        "v": pltpu.VMEM((tokens, total_width), bf16),
        "code": pltpu.VMEM((code_shape[1], code_shape[0], tokens), jnp.int32),
        "g": pltpu.VMEM((tokens, total_width), bf16),
        **{n: dma((chunks, SUBS)) for n in ("f1s", "f1r")},
        **{n: dma((2, SUBS)) for n in (
            "f2s", "f2r", "agms", "agmr", "f3r", "agts", "agtr", "b2s", "b2r", "agbs", "agbr")},
        "f3s": dma((2, 2, SUBS)),
        **{n: dma((3, SUBS)) for n in ("b1s", "b1r")},
        **{n: dma((2,)) for n in ("u1s", "u1r", "u2s", "u2r", "w0s", "w0r")},
        **{n: dma((2, n_head - 1)) for n in ("hs_", "hr_")},
        "load": dma((5,)),
        "entry": pltpu.SemaphoreType.REGULAR,
    }


def on_line(n_head, queries, keys, values, level_codes, cotangent):
    tokens, depth = queries.shape
    total_width = values.shape[1]
    rows = tokens // n_head
    f32, bf16 = jnp.float32, jnp.bfloat16
    vmem = pl.BlockSpec(memory_space=pltpu.VMEM)
    scratch = line_scratch(tokens, depth, total_width, level_codes.shape, n_head)
    results = pl.pallas_call(
        functools.partial(line_kernel, n_head, tuple(scratch)),
        out_shape=(
            *[jax.ShapeDtypeStruct((tokens // PIECES, total_width), bf16)] * (2 * PIECES),
            jax.ShapeDtypeStruct((rows, depth), f32),
            jax.ShapeDtypeStruct((rows, depth), f32),
        ),
        in_specs=[pl.BlockSpec(memory_space=pltpu.HBM)] * 5,
        out_specs=(vmem,) * (2 * PIECES + 2),
        scratch_shapes=list(scratch.values()),
        compiler_params=pltpu.CompilerParams(
            collective_id=1, has_side_effects=True, vmem_limit_bytes=ROOM),
    )(queries, keys, values, jnp.transpose(level_codes, (1, 0, 2)), cotangent)
    return hand_over(tokens, total_width, results)


def per_device(n_seq, n_head, queries, keys, values, level_codes, cotangent):
    suits = n_seq == 8 and n_head == 4 and values.shape[1] == 4 * LANES and queries.shape[0] == 2 * STRETCH
    if suits:
        return on_line(n_head, queries, keys, values, level_codes, cotangent)
    return on_any(n_seq, n_head, queries, keys, values, level_codes, cotangent)


def solution(mesh):
    placed = (
        P("seq", None),
        P("seq", None),
        P("seq", "head"),
        P("head", None, "seq"),
        P("seq", "head"),
    )
    return jax.shard_map(
        functools.partial(per_device, mesh.shape["seq"], mesh.shape["head"]),
        mesh=mesh,
        in_specs=placed,
        out_specs=(
            P("seq", "head"),
            P(("seq", "head"), None),
            P(("seq", "head"), None),
            P("seq", "head"),
        ),
        check_vma=False,
    )
```

```python
import functools

import jax
import jax.numpy as jnp
from jax import lax
from jax.experimental import pallas as pl
from jax.experimental.pallas import tpu as pltpu
from jax.sharding import PartitionSpec as P

STRETCH_BITS = 7
STRETCH = 128
LANES = 128
SCALE_CODE = 0.125
MESH = pl.DeviceIdType.MESH
PIECES = 8
ROOM = 54656 * 1024


def dot(a, b, da, db):
    return lax.dot_general(a, b, (((da,), (db,)), ((), ())), preferred_element_type=jnp.float32)


def kernel(
    n_seq, n_head,
    q_in, k_in, v_in, code_in, g_in,
    *rest,
):
    att_outs, vg_outs = rest[:PIECES], rest[PIECES:2 * PIECES]
    (
    qg_out, kg_out,
    att, vg, qg, kg, wts, lams, own, got, pend, back, racc, qk_send, qk_recv,
    f_send, f_recv, b_send, b_recv, h_send, h_recv,
    q_ref, k_ref, v_ref, code_ref, g_ref, load) = rest[2 * PIECES:]
    loads = [
        pltpu.make_async_copy(src, dst, load.at[i])
        for i, (src, dst) in enumerate((
            (k_in, k_ref), (v_in, v_ref), (g_in, g_ref), (q_in, q_ref), (code_in, code_ref)))
    ]
    for one in loads:
        one.start()
    tokens, depth = q_ref.shape
    total_width = v_ref.shape[1]
    heads = code_ref.shape[1]
    width = total_width // heads
    chunks = total_width // LANES
    per_chunk = LANES // width
    blocks = tokens // STRETCH
    rows = tokens // n_head
    bits = n_seq.bit_length() - 1
    scale = depth ** -0.5
    near = STRETCH_BITS + 1
    far = near + 1
    f32, bf16 = jnp.float32, jnp.bfloat16
    seq, head = lax.axis_index("seq"), lax.axis_index("head")
    bit = [lax.rem(lax.div(seq, 1 << b), 2) for b in range(bits)]
    low_bits = bits - 2
    top, mid = bits - 1, bits - 2
    stride = 1 << mid
    line = lax.div(seq, stride)
    partner = [seq + (1 << b) * (1 - 2 * bit[b]) for b in range(low_bits)]
    peers = [lax.rem(head + j, n_head) for j in range(1, n_head)]

    barrier = pltpu.get_barrier_semaphore()

    def greet(to):
        pl.semaphore_signal(barrier, inc=1, device_id=to, device_id_type=MESH)

    for b in range(low_bits):
        greet((partner[b], head))
    for peer in peers:
        greet((seq, peer))

    @pl.when(line > 0)
    def _():
        greet((seq - stride, head))

    @pl.when(line < 3)
    def _():
        greet((seq + stride, head))

    greetings = low_bits + n_head - 1 + (line > 0).astype(jnp.int32) + (line < 3).astype(jnp.int32)

    def forward(b, c, relay=False):
        return pltpu.make_async_remote_copy(
            src_ref=(got if relay else own).at[b, c], dst_ref=got.at[b, c],
            send_sem=f_send.at[b, c], recv_sem=f_recv.at[b, c],
            device_id=(partner[b] if b < low_bits else seq + stride, head), device_id_type=MESH)

    def backward(b, c):
        return pltpu.make_async_remote_copy(
            src_ref=pend.at[b, c], dst_ref=back.at[b, c],
            send_sem=b_send.at[b, c], recv_sem=b_recv.at[b, c],
            device_id=(partner[b] if b < low_bits else seq - stride, head), device_id_type=MESH)

    highest = [lax.div(seq, 2 << b) == (n_seq >> (b + 1)) - 1 for b in range(low_bits)]
    up_sends = [jnp.logical_or(bit[b] == 0, jnp.logical_not(highest[b])) for b in range(low_bits)]
    up_gets = [jnp.logical_or(bit[b] == 1, jnp.logical_not(highest[b])) for b in range(low_bits)]
    down_sends, down_gets = up_gets, up_sends

    cols = [slice(c * LANES, (c + 1) * LANES) for c in range(chunks)]

    spread = (
        lax.broadcasted_iota(jnp.int32, (heads, total_width), 1) // width
        == lax.broadcasted_iota(jnp.int32, (heads, total_width), 0)
    ).astype(f32)

    def level_weights(level):
        lam = code_ref[level].astype(f32) * SCALE_CODE
        return dot(lam, spread, 0, 0)

    def prepare(b):
        @pl.when(bit[b] == 1)
        def _():
            lam = level_weights(far + b)
            lams[b] = lam.astype(bf16)
            weighted = (g_ref[...].astype(f32) * lam).astype(bf16)
            wts[b] = weighted
            sending = dot(q_ref[...], weighted, 0, 0) * scale
            for c in range(chunks):
                pend[b, c] = sending[:, cols[c]]

        if b < low_bits:
            @pl.when(bit[b] == 0)
            def _():
                for c in range(chunks):
                    pend[b, c] = jnp.zeros((depth, LANES), f32)

    first_half = slice(0, STRETCH)
    second_half = slice(STRETCH, 2 * STRETCH)
    loads[0].wait()
    loads[1].wait()
    state_low = dot(k_ref[first_half, :], v_ref[first_half, :], 0, 0)
    state_all = state_low + dot(k_ref[second_half, :], v_ref[second_half, :], 0, 0)
    for c in range(chunks):
        own[0, c] = state_all[:, cols[c]]
    pl.semaphore_wait(barrier, greetings)
    for c in range(chunks):
        @pl.when(up_sends[0])
        def _(c=c):
            forward(0, c).start()
    for one in loads[2:]:
        one.wait()
    prepare(top)
    for c in range(chunks):
        @pl.when(line == 3)
        def _(c=c):
            backward(top, c).start()
    prepare(mid)
    for c in range(chunks):
        @pl.when(line == 3)
        def _(c=c):
            backward(mid, c).start()
    for b in range(low_bits - 1, -1, -1):
        prepare(b)

    key_pos = lax.rem(lax.broadcasted_iota(jnp.int32, (per_chunk * STRETCH, STRETCH), 0), STRETCH)
    query_pos = lax.broadcasted_iota(jnp.int32, (per_chunk * STRETCH, STRETCH), 1)
    differ = jnp.bitwise_xor(query_pos, key_pos)
    causal = key_pos <= query_pos
    lane_head = lax.broadcasted_iota(jnp.int32, (STRETCH, LANES), 1) // width

    def split_heads(block):
        block = block.astype(f32)
        return jnp.concatenate(
            [jnp.where(lane_head == i, block, 0.0) for i in range(per_chunk)], axis=0).astype(bf16)

    press_sum = [jnp.zeros((STRETCH, STRETCH), f32) for _ in range(blocks)]
    scores = []
    for n in range(blocks):
        at = slice(n * STRETCH, (n + 1) * STRETCH)
        one = dot(k_ref[at, :], q_ref[at, :], 1, 1) * scale
        scores.append(jnp.concatenate([one] * per_chunk, axis=0))

    def unit(n, c):
        at = slice(n * STRETCH, (n + 1) * STRETCH)

        def rows_of(level):
            parts = []
            for i in range(per_chunk):
                row = code_ref[level, c * per_chunk + i:c * per_chunk + i + 1, at].astype(f32) * SCALE_CODE
                parts.append(jnp.broadcast_to(row, (STRETCH, STRETCH)))
            return jnp.concatenate(parts, axis=0)

        mask = rows_of(STRETCH_BITS)
        for level in range(STRETCH_BITS - 1, -1, -1):
            mask = jnp.where(differ < (1 << level), rows_of(level), mask)
        mask = jnp.where(causal, mask, 0.0)
        mixed = (scores[n] * mask).astype(bf16)
        v_split = split_heads(v_ref[at, cols[c]])
        g_block = g_ref[at, cols[c]]
        att[at, cols[c]] = dot(mixed, v_split, 0, 0)
        wide = jnp.concatenate(
            [mixed[i * STRETCH:(i + 1) * STRETCH] for i in range(per_chunk)], axis=1)
        vg[at, cols[c]] = dot(wide, split_heads(g_block), 1, 0)
        press = dot(v_split, g_block, 1, 1) * mask
        for i in range(per_chunk):
            press_sum[n] = press_sum[n] + press[i * STRETCH:(i + 1) * STRETCH]

    def finish_block(n):
        at = slice(n * STRETCH, (n + 1) * STRETCH)
        press = press_sum[n].astype(bf16)
        qg[at, :] = dot(press, k_ref[at, :], 0, 0) * scale
        kg[at, :] = dot(press, q_ref[at, :], 1, 0) * scale

    def near_level():
        low = state_low.astype(bf16)
        lam = level_weights(near)[second_half]
        att[second_half, :] = att[second_half, :] + lam * (
            dot(q_ref[second_half, :], low, 1, 0) * scale)
        weighted = (g_ref[second_half, :].astype(f32) * lam).astype(bf16)
        qg[second_half, :] = qg[second_half, :] + dot(weighted, low, 1, 1) * scale
        return dot(q_ref[second_half, :], weighted, 0, 0) * scale

    def consume(b):
        @pl.when(bit[b] == 1)
        def _():
            total = jnp.zeros((tokens, depth), f32)
            for c in range(chunks):
                state = got[b, c].astype(bf16)
                reading = dot(q_ref[...], state, 1, 0) * scale
                att[:, cols[c]] = att[:, cols[c]] + reading * lams[b, :, cols[c]].astype(f32)
                total = total + dot(wts[b, :, cols[c]], state, 1, 1)
            qg[...] = qg[...] + total * scale

    def share(which, j):
        return pltpu.make_async_remote_copy(
            src_ref=qk_send.at[which, peers[j]], dst_ref=qk_recv.at[which, j],
            send_sem=h_send.at[which, j], recv_sem=h_recv.at[which, j],
            device_id=(seq, peers[j]), device_id_type=MESH)

    def send_share(which, grad):
        for i in range(n_head):
            qk_send[which, i] = grad[i * rows:(i + 1) * rows]
        for j in range(n_head - 1):
            share(which, j).start()

    def step_forward(stage, c):
        if stage < low_bits:
            b = stage

            @pl.when(up_gets[b])
            def _():
                forward(b, c).wait_recv()
                own[b + 1, c] = own[b, c] + got[b, c]

            if b + 1 < low_bits:
                @pl.when(up_sends[b + 1])
                def _():
                    forward(b + 1, c).start()
            else:
                @pl.when(bit[mid] == 0)
                def _():
                    forward(mid, c).start()
        elif stage == low_bits:
            @pl.when(bit[mid] == 1)
            def _():
                forward(mid, c).wait_recv()

            @pl.when(line == 1)
            def _():
                own[top, c] = own[mid, c] + got[mid, c]
                forward(top, c).start()
        elif stage == low_bits + 1:
            @pl.when(line == 2)
            def _():
                forward(top, c).wait_recv()
                forward(top, c, True).start()
        else:
            @pl.when(line == 3)
            def _():
                forward(top, c).wait_recv()

    def pass_down(b, c):
        pend[b, c] = pend[b, c] + racc[c]

        @pl.when(down_sends[b])
        def _():
            backward(b, c).start()

    def step_backward(stage, c):
        if stage == 0:
            @pl.when(line == 2)
            def _():
                backward(top, c).wait_recv()
                pend[top, c] = pend[top, c] + back[top, c]
                backward(top, c).start()

            @pl.when(line == 3)
            def _():
                racc[c] = jnp.zeros((depth, LANES), f32)
                pass_down(low_bits - 1, c)
        elif stage == 1:
            @pl.when(line == 1)
            def _():
                backward(top, c).wait_recv()
                pend[mid, c] = pend[mid, c] + back[top, c]
                backward(mid, c).start()
                racc[c] = back[top, c]
                pass_down(low_bits - 1, c)

            @pl.when(line == 2)
            def _():
                backward(mid, c).wait_recv()
                racc[c] = back[mid, c]
                pass_down(low_bits - 1, c)
        elif stage == 2:
            @pl.when(line == 0)
            def _():
                backward(mid, c).wait_recv()
                racc[c] = back[mid, c]
                pass_down(low_bits - 1, c)
        else:
            b = low_bits - 1 - (stage - 3)

            @pl.when(down_gets[b])
            def _():
                backward(b, c).wait_recv()
                racc[c] = racc[c] + back[b, c]

            if b > 0:
                pass_down(b - 1, c)

    near_sum = None
    stages = low_bits + 3
    for c in range(chunks):
        unit(0, c)
    finish_block(0)
    for c in range(chunks):
        step_backward(0, c)
        step_forward(0, c)
    for stage in range(1, low_bits):
        for c in range(chunks):
            step_forward(stage, c)
    for c in range(chunks):
        step_backward(1, c)
        step_forward(low_bits, c)
    for c in range(chunks):
        step_backward(2, c)
        step_forward(low_bits + 1, c)
    for c in range(chunks):
        unit(1, c)
    finish_block(1)
    near_sum = near_level()
    for b in range(low_bits):
        consume(b)
    consume(mid)
    for c in range(chunks):
        step_forward(low_bits + 2, c)
    consume(top)
    send_share(0, qg[...])
    part = tokens // PIECES
    for p in range(PIECES):
        att_outs[p][...] = att[p * part:(p + 1) * part, :].astype(bf16)
    for stage in range(3, stages):
        for c in range(chunks):
            step_backward(stage, c)

    grad_low = kg[first_half, :]
    grad_high = kg[second_half, :]
    for c in range(chunks):
        incoming = racc[c]
        low = (incoming + near_sum[:, cols[c]]).astype(bf16)
        high = incoming.astype(bf16)
        grad_low = grad_low + dot(v_ref[first_half, cols[c]], low, 1, 1)
        grad_high = grad_high + dot(v_ref[second_half, cols[c]], high, 1, 1)
    send_share(1, jnp.concatenate([grad_low, grad_high], axis=0))
    for c in range(chunks):
        incoming = racc[c]
        low = (incoming + near_sum[:, cols[c]]).astype(bf16)
        high = incoming.astype(bf16)
        for half, state in ((first_half, low), (second_half, high)):
            final = (vg[half, cols[c]] + dot(k_ref[half, :], state, 1, 0)).astype(bf16)
            for p in range(PIECES // 2):
                vg_outs[half.start // part + p][:, cols[c]] = final[p * part:(p + 1) * part]

    for which, out in ((0, qg_out), (1, kg_out)):
        total = qk_send[which, head]
        for j in range(n_head - 1):
            share(which, j).wait_recv()
            total = total + qk_recv[which, j]
        out[...] = total
    for which in range(2):
        for j in range(n_head - 1):
            share(which, j).wait_send()
    for c in range(chunks):
        for b in range(low_bits):
            @pl.when(up_sends[b])
            def _(b=b, c=c):
                forward(b, c).wait_send()

            @pl.when(down_sends[b])
            def _(b=b, c=c):
                backward(b, c).wait_send()

        @pl.when(bit[mid] == 0)
        def _(c=c):
            forward(mid, c).wait_send()

        @pl.when(bit[mid] == 1)
        def _(c=c):
            backward(mid, c).wait_send()

        @pl.when(line == 1)
        def _(c=c):
            forward(top, c).wait_send()

        @pl.when(line == 2)
        def _(c=c):
            forward(top, c, True).wait_send()

        @pl.when(line >= 2)
        def _(c=c):
            backward(top, c).wait_send()


def on_any(n_seq, n_head, queries, keys, values, level_codes, cotangent):
    tokens, depth = queries.shape
    total_width = values.shape[1]
    chunks = total_width // LANES
    rows = tokens // n_head
    bits = n_seq.bit_length() - 1
    f32, bf16 = jnp.float32, jnp.bfloat16
    vmem = pl.BlockSpec(memory_space=pltpu.VMEM)
    links = (bits, chunks, depth, LANES)
    dma = pltpu.SemaphoreType.DMA
    results = pl.pallas_call(
        functools.partial(kernel, n_seq, n_head),
        out_shape=(
            *[jax.ShapeDtypeStruct((tokens // PIECES, total_width), bf16)] * (2 * PIECES),
            jax.ShapeDtypeStruct((rows, depth), f32),
            jax.ShapeDtypeStruct((rows, depth), f32),
        ),
        in_specs=[pl.BlockSpec(memory_space=pltpu.HBM)] * 5,
        out_specs=(vmem,) * (2 * PIECES + 2),
        scratch_shapes=[
            pltpu.VMEM((tokens, total_width), f32),
            pltpu.VMEM((tokens, total_width), f32),
            pltpu.VMEM((tokens, depth), f32),
            pltpu.VMEM((tokens, depth), f32),
            pltpu.VMEM((bits, tokens, total_width), bf16),
            pltpu.VMEM((bits, tokens, total_width), bf16),
            pltpu.VMEM(links, f32),
            pltpu.VMEM(links, f32),
            pltpu.VMEM(links, f32),
            pltpu.VMEM(links, f32),
            pltpu.VMEM((chunks, depth, LANES), f32),
            pltpu.VMEM((2, n_head, rows, depth), f32),
            pltpu.VMEM((2, n_head - 1, rows, depth), f32),
            dma((bits, chunks)),
            dma((bits, chunks)),
            dma((bits, chunks)),
            dma((bits, chunks)),
            dma((2, n_head - 1)),
            dma((2, n_head - 1)),
            pltpu.VMEM((tokens, depth), bf16),
            pltpu.VMEM((tokens, depth), bf16),
            pltpu.VMEM((tokens, total_width), bf16),
            pltpu.VMEM((level_codes.shape[1], level_codes.shape[0], tokens), jnp.int32),
            pltpu.VMEM((tokens, total_width), bf16),
            dma((5,)),
        ],
        compiler_params=pltpu.CompilerParams(
            collective_id=0, has_side_effects=True, vmem_limit_bytes=ROOM),
    )(queries, keys, values, jnp.transpose(level_codes, (1, 0, 2)), cotangent)
    return hand_over(tokens, total_width, results)


def settle(*refs):
    att_parts, vg_parts = refs[:PIECES], refs[PIECES:2 * PIECES]
    qg, kg, att_out, qg_out, kg_out, vg_out, sems = refs[2 * PIECES:]
    part = att_parts[0].shape[0]
    pairs = [(qg, qg_out), (kg, kg_out)]
    for p in range(PIECES):
        pairs.append((att_parts[p], att_out.at[pl.ds(p * part, part)]))
        pairs.append((vg_parts[p], vg_out.at[pl.ds(p * part, part)]))
    copies = [pltpu.make_async_copy(a, b, sems.at[i]) for i, (a, b) in enumerate(pairs)]
    for one in copies:
        one.start()
    for one in copies:
        one.wait()


def hand_over(tokens, total_width, results):
    wide = jax.ShapeDtypeStruct((tokens, total_width), jnp.bfloat16)
    thin = jax.ShapeDtypeStruct(results[-1].shape, jnp.float32)
    anywhere = pl.BlockSpec(memory_space=pl.ANY)
    return pl.pallas_call(
        settle,
        out_shape=(wide, thin, thin, wide),
        in_specs=[anywhere] * len(results),
        out_specs=(anywhere,) * 4,
        scratch_shapes=[pltpu.SemaphoreType.DMA((len(results),))],
        compiler_params=pltpu.CompilerParams(vmem_limit_bytes=1024 * 1024),
    )(*results)


SUBS = 2
AHEAD = (3, 2, 1)


def line_kernel(n_head, names, q_in, k_in, v_in, code_in, g_in, *rest):
    att_outs, vg_outs = rest[:PIECES], rest[PIECES:2 * PIECES]
    qg_out, kg_out = rest[2 * PIECES:2 * PIECES + 2]
    r = dict(zip(names, rest[2 * PIECES + 2:]))
    att, vg, qg, kg, wts, lams = (r[n] for n in ("att", "vg", "qg", "kg", "wts", "lams"))
    own, sx, rr, gm, tt, gt = (r[n] for n in ("own", "sx", "rr", "gm", "tt", "gt"))
    w0, wmid, wtop, rz, zz, gz = (r[n] for n in ("w0", "wmid", "wtop", "rz", "zz", "gz"))
    gu, g0, hb, hs, hx = (r[n] for n in ("gu", "g0", "hb", "hs", "hx"))
    es = r["es"]
    nearby, qk_send, qk_recv = (r[n] for n in ("nearby", "qk_send", "qk_recv"))
    q_ref, k_ref, v_ref, code_ref, g_ref = (r[n] for n in ("q", "k", "v", "code", "g"))
    load, entry = r["load"], r["entry"]

    loads = [
        pltpu.make_async_copy(src, dst, load.at[i])
        for i, (src, dst) in enumerate((
            (k_in, k_ref), (v_in, v_ref), (g_in, g_ref), (q_in, q_ref), (code_in, code_ref)))
    ]
    for one in loads:
        one.start()
    tokens, depth = q_ref.shape
    total_width = v_ref.shape[1]
    heads = code_ref.shape[1]
    width = total_width // heads
    chunks = total_width // LANES
    per_chunk = LANES // width
    blocks = tokens // STRETCH
    share_rows = tokens // n_head
    scale = depth ** -0.5
    near = STRETCH_BITS + 1
    far = near + 1
    top, mid = 2, 1
    half_width = total_width // 2
    f32, bf16 = jnp.float32, jnp.bfloat16
    seq, head = lax.axis_index("seq"), lax.axis_index("head")
    x = lax.rem(seq, 2)
    line = lax.div(seq, 2)
    low = lax.rem(line, 2)
    across = seq + 1 - 2 * x
    first = x + low * (1 - 2 * x)
    peers = [lax.rem(head + j, n_head) for j in range(1, n_head)]

    def when(*conditions):
        return pl.when(functools.reduce(jnp.logical_and, conditions))

    left, right = x == 0, x == 1
    early, late = line < 2, line >= 2
    even, odd = low == 0, low == 1
    barrier = pltpu.get_barrier_semaphore()

    def greet(to, sem=barrier):
        pl.semaphore_signal(sem, inc=1, device_id=to, device_id_type=MESH)

    greet((across, head))
    for peer in peers:
        greet((seq, peer))

    @when(line == 0)
    def _():
        greet((seq + 2, head))

    @when(early)
    def _():
        greet((x + 4, head))
        greet((x + 6, head))

    @when(line == 1)
    def _():
        greet((7 - x, head))

    @when(late)
    def _():
        greet((seq + 2 - 4 * low, head))
        greet((across + 2 - 4 * low, head))

    def rows(s):
        return pl.ds(s * (depth // SUBS), depth // SUBS)

    subs = [(j, s) for j in range(2) for s in range(SUBS)]

    def mine(j):
        return 2 * x + j

    def other(j):
        return 2 * (1 - x) + j

    def remote(src, dst, send, recv, to):
        return pltpu.make_async_remote_copy(
            src_ref=src, dst_ref=dst, send_sem=send, recv_sem=recv,
            device_id=(to, head), device_id_type=MESH)

    def f1(c, s):
        return remote(own.at[c, rows(s)], sx.at[c, rows(s)],
                      r["f1s"].at[c, s], r["f1r"].at[c, s], across)

    def f2(c, s):
        return remote(rr.at[c, rows(s)], gm.at[c, rows(s)],
                      r["f2s"].at[c, s], r["f2r"].at[c, s], seq + 2)

    def agm(c, j, s):
        return remote(gm.at[c, rows(s)], gm.at[c, rows(s)],
                      r["agms"].at[j, s], r["agmr"].at[j, s], across)

    def f3(d, j, s):
        return remote(tt.at[j, rows(s)], gt.at[mine(j), rows(s)],
                      r["f3s"].at[d, j, s], r["f3r"].at[j, s], seq + 2 if d == 1 else across + 4)

    def agt(c, j, s):
        return remote(gt.at[c, rows(s)], gt.at[c, rows(s)],
                      r["agts"].at[j, s], r["agtr"].at[j, s], seq + 2 - 4 * low)

    def b1(i, s):
        there_x = x if i % 2 == 0 else 1 - x
        there_low = low if i < 2 else 1 - low
        to = seq + (there_x - x) + 2 * (there_low - low)
        return remote(wtop.at[2 * there_x + there_low, rows(s)], rz.at[i - 1, rows(s)],
                      r["b1s"].at[i - 1, s], r["b1r"].at[i - 1, s], to)

    def b2(d, j, s):
        return remote(zz.at[rows(s)], gz.at[j, rows(s)],
                      r["b2s"].at[d, s], r["b2r"].at[j, s], x + 2 * d)

    def raw(c):
        return remote(wmid.at[c], gu.at[c], r["us_"].at[c], r["ur_"].at[c], seq - 2)

    def e1(j):
        return remote(es.at[j], g0.at[j], r["e1s"].at[j], r["e1r"].at[j], across)

    def agb(j, s):
        return remote(hs.at[j, rows(s)], hx.at[j, rows(s)],
                      r["agbs"].at[j, s], r["agbr"].at[j, s], across)

    def share(which, j):
        return pltpu.make_async_remote_copy(
            src_ref=qk_send.at[which, peers[j]], dst_ref=qk_recv.at[which, j],
            send_sem=r["hs_"].at[which, j], recv_sem=r["hr_"].at[which, j],
            device_id=(seq, peers[j]), device_id_type=MESH)

    def send_share(which, grad):
        for i in range(n_head):
            qk_send[which, i] = grad[i * share_rows:(i + 1) * share_rows]
        for j in (1, 2, 0) if n_head == 4 else range(n_head - 1):
            share(which, j).start()

    cols = [slice(c * LANES, (c + 1) * LANES) for c in range(chunks)]
    spread = (
        lax.broadcasted_iota(jnp.int32, (heads, total_width), 1) // width
        == lax.broadcasted_iota(jnp.int32, (heads, total_width), 0)
    ).astype(f32)

    def level_weights(level):
        lam = code_ref[level].astype(f32) * SCALE_CODE
        return dot(lam, spread, 0, 0)

    def prepare(b, into):
        lam = level_weights(far + b)
        lams[b] = lam.astype(bf16)
        weighted = (g_ref[...].astype(f32) * lam).astype(bf16)
        wts[b] = weighted
        sending = dot(q_ref[...], weighted, 0, 0) * scale
        for c in range(chunks):
            into[c] = sending[:, cols[c]]

    first_half = slice(0, STRETCH)
    second_half = slice(STRETCH, 2 * STRETCH)
    for one in loads:
        one.wait()

    @when(late)
    def _():
        prepare(top, wtop)

        @when(line == 2)
        def _():
            pl.semaphore_wait(barrier, n_head + 4)

        @when(line == 3)
        def _():
            pl.semaphore_wait(barrier, n_head + 5)
        for s in range(SUBS):
            for i in AHEAD:
                b1(i, s).start()
        greet((first + 2, head), entry)

    state_low = dot(k_ref[first_half, :], v_ref[first_half, :], 0, 0)
    state_all = state_low + dot(k_ref[second_half, :], v_ref[second_half, :], 0, 0)
    for c in range(chunks):
        own[c] = state_all[:, cols[c]]

    @when(line == 0)
    def _():
        pl.semaphore_wait(barrier, n_head)

    @when(line == 1)
    def _():
        pl.semaphore_wait(barrier, n_head + 1)
        greet((x, head), entry)

    @when(early)
    def _():
        for j, s in subs:
            f1(other(j), s).start()

    @when(early, jnp.logical_or(line == 0, left))
    def _():
        for j, s in subs:
            f1(mine(j), s).start()

    @when(odd)
    def _():
        prepare(mid, wmid)

    @when(line == 1)
    def _():
        for half in (other, mine):
            for j in range(2):
                raw(half(j)).start()

    @when(right)
    def _():
        prepare(0, w0)

        @when(odd)
        def _():
            for j in range(2):
                es[j] = w0[j]

    key_pos = lax.rem(lax.broadcasted_iota(jnp.int32, (per_chunk * STRETCH, STRETCH), 0), STRETCH)
    query_pos = lax.broadcasted_iota(jnp.int32, (per_chunk * STRETCH, STRETCH), 1)
    differ = jnp.bitwise_xor(query_pos, key_pos)
    causal = key_pos <= query_pos
    lane_head = lax.broadcasted_iota(jnp.int32, (STRETCH, LANES), 1) // width

    def split_heads(block):
        block = block.astype(f32)
        return jnp.concatenate(
            [jnp.where(lane_head == i, block, 0.0) for i in range(per_chunk)], axis=0).astype(bf16)

    def do_block(n):
        at = slice(n * STRETCH, (n + 1) * STRETCH)
        one = dot(k_ref[at, :], q_ref[at, :], 1, 1) * scale
        scores = jnp.concatenate([one] * per_chunk, axis=0)
        press_sum = jnp.zeros((STRETCH, STRETCH), f32)
        for c in range(chunks):
            def rows_of(level):
                parts = []
                for i in range(per_chunk):
                    row = code_ref[level, c * per_chunk + i:c * per_chunk + i + 1, at].astype(f32) * SCALE_CODE
                    parts.append(jnp.broadcast_to(row, (STRETCH, STRETCH)))
                return jnp.concatenate(parts, axis=0)

            mask = rows_of(STRETCH_BITS)
            for level in range(STRETCH_BITS - 1, -1, -1):
                mask = jnp.where(differ < (1 << level), rows_of(level), mask)
            mask = jnp.where(causal, mask, 0.0)
            mixed = (scores * mask).astype(bf16)
            v_split = split_heads(v_ref[at, cols[c]])
            g_block = g_ref[at, cols[c]]
            att[at, cols[c]] = dot(mixed, v_split, 0, 0)
            wide = jnp.concatenate(
                [mixed[i * STRETCH:(i + 1) * STRETCH] for i in range(per_chunk)], axis=1)
            vg[at, cols[c]] = dot(wide, split_heads(g_block), 1, 0)
            press = dot(v_split, g_block, 1, 1) * mask
            for i in range(per_chunk):
                press_sum = press_sum + press[i * STRETCH:(i + 1) * STRETCH]
        press_sum = press_sum.astype(bf16)
        qg[at, :] = dot(press_sum, k_ref[at, :], 0, 0) * scale
        kg[at, :] = dot(press_sum, q_ref[at, :], 1, 0) * scale

    def near_level():
        state = state_low.astype(bf16)
        lam = level_weights(near)[second_half]
        att[second_half, :] = att[second_half, :] + lam * (
            dot(q_ref[second_half, :], state, 1, 0) * scale)
        weighted = (g_ref[second_half, :].astype(f32) * lam).astype(bf16)
        qg[second_half, :] = qg[second_half, :] + dot(weighted, state, 1, 1) * scale
        nearby[...] = dot(q_ref[second_half, :], weighted, 0, 0) * scale

    def span(side):
        return pl.ds(pl.multiple_of(side * half_width, half_width), half_width)

    def read_state(b, side, ref):
        at = span(side)
        state = jnp.concatenate([ref[2 * side], ref[2 * side + 1]], axis=1).astype(bf16)
        reading = dot(q_ref[...], state, 1, 0) * scale
        total = att[:, at] + reading * lams[b, :, at].astype(f32)
        qg[...] = qg[...] + dot(wts[b, :, at], state, 1, 1) * scale
        return total

    def consume(b, side, ref):
        att[:, span(side)] = read_state(b, side, ref)

    part = tokens // PIECES

    def write_att(side, total):
        total = total.astype(bf16)
        for p in range(PIECES):
            att_outs[p][:, span(side)] = total[p * part:(p + 1) * part]

    def take_incoming(side, pair):
        at = span(side)
        incoming = jnp.concatenate(pair, axis=1)
        for half, state in (
                (first_half, incoming + nearby[:, at]), (second_half, incoming)):
            state = state.astype(bf16)
            kg[half, :] = kg[half, :] + dot(v_ref[half, at], state, 1, 1)
            final = (vg[half, at] + dot(k_ref[half, :], state, 1, 0)).astype(bf16)
            for p in range(PIECES // 2):
                vg_outs[half.start // part + p][:, at] = final[p * part:(p + 1) * part]

    do_block(0)

    @when(line == 2)
    def _():
        for j, s in subs:
            f1(other(j), s).start()

    @when(left, line == 2)
    def _():
        for j, s in subs:
            f1(mine(j), s).start()

    @when(left, line == 3)
    def _():
        for half in (0, 2):
            for j, s in subs:
                f1(half + j, s).start()

    @when(line == 3)
    def _():
        for j in range(2):
            raw(other(j)).start()

    @when(right, line == 3)
    def _():
        for j in range(2):
            e1(j).start()

    @when(late)
    def _():
        for s in range(SUBS):
            for i in AHEAD:
                b1(i, s).wait_recv()
            zz[rows(s)] = (wtop[mine(low), rows(s)] + rz[0, rows(s)]) + (
                rz[1, rows(s)] + rz[2, rows(s)])
            b2(0, low, s).start()
        for s in range(SUBS):
            b2(1, low, s).start()

    @when(line == 0)
    def _():
        pl.semaphore_wait(entry, 1)

    def add_near(j, s):
        f1(mine(j), s).wait_recv()
        rr[mine(j), rows(s)] = own[mine(j), rows(s)] + sx[mine(j), rows(s)]

    @when(early)
    def _():
        for j, s in subs:
            add_near(j, s)

            @when(line == 0)
            def _():
                f2(mine(j), s).start()

    @when(line == 3)
    def _():
        for j in range(2):
            raw(mine(j)).start()

        @when(right)
        def _():
            for j, s in subs:
                hs[j, rows(s)] = w0[2 + j, rows(s)]
                hx[j, rows(s)] = jnp.zeros((depth // SUBS, LANES), f32)
                agb(j, s).start()

    @when(right, line == 1)
    def _():
        for j in range(2):
            e1(j).start()

    do_block(1)
    near_level()

    @when(line == 1)
    def _():
        pl.semaphore_wait(entry, 2)
        for j, s in subs:
            f2(mine(j), s).wait_recv()
            tt[j, rows(s)] = gm[mine(j), rows(s)] + rr[mine(j), rows(s)]
            f3(1, j, s).start()
        for j, s in subs:
            f3(0, j, s).start()

    def pass_raw():
        for j in range(2):
            raw(other(j)).wait_recv()

            @when(left)
            def _():
                es[j] = gu[2 + j]

            @when(right)
            def _():
                es[j] = gu[j] + w0[j]
            e1(j).start()

    @when(line == 0)
    def _():
        pass_raw()

    @when(line == 2)
    def _():
        for j, s in subs:
            add_near(j, s)
            f2(mine(j), s).start()

    @when(line == 0)
    def _():
        for j, s in subs:
            f1(other(j), s).wait_recv()
            rr[other(j), rows(s)] = own[other(j), rows(s)] + sx[other(j), rows(s)]
            f2(other(j), s).start()

    @when(line == 2)
    def _():
        pass_raw()

    def read_neighbour():
        @when(right, jnp.logical_or(line == 1, line == 2))
        def _():
            for j, s in subs:
                f1(j, s).wait_recv()

        @when(right, line == 3)
        def _():
            for c in range(chunks):
                for s in range(SUBS):
                    f1(c, s).wait_recv()

        @when(right)
        def _():
            consume(0, 0, sx)
            consume(0, 1, sx)

    def read_mid():
        @when(line == 1)
        def _():
            for j, s in subs:
                f2(other(j), s).wait_recv()

        @when(line == 3)
        def _():
            for j, s in subs:
                agm(other(j), j, s).wait_recv()
        consume(mid, 0, gm)
        consume(mid, 1, gm)

    def pass_across(j, s, total):
        hb[j, rows(s)] = total

        @when(left)
        def _():
            hs[j, rows(s)] = total

        @when(right)
        def _():
            hs[j, rows(s)] = total + w0[2 + j, rows(s)]

        agb(j, s).start()

    def take_own():
        @when(jnp.logical_or(left, even))
        def _():
            for j in range(2):
                e1(j).wait_recv()
                hb[j] = hb[j] + g0[j]
        take_incoming(x, [hb[0], hb[1]])

    def take_other():
        for j, s in subs:
            agb(j, s).wait_recv()

        @when(even)
        def _():
            for j in range(2):
                hx[j] = hx[j] + gu[other(j)]
        take_incoming(1 - x, [hx[0], hx[1]])

    @when(early)
    def _():
        read_neighbour()

        @when(line == 1)
        def _():
            read_mid()

        send_share(0, qg[...])
        write_att(0, att[:, :half_width])
        write_att(1, att[:, half_width:])

        @when(line == 0)
        def _():
            for j in range(2):
                raw(mine(j)).wait_recv()
        for j, s in subs:
            b2(0, j, s).wait_recv()

            @when(line == 0)
            def _():
                gz[j, rows(s)] = gz[j, rows(s)] + gu[mine(j), rows(s)]
            pass_across(j, s, gz[j, rows(s)])
        take_own()
        take_other()
        send_share(1, kg[...])

    @when(late)
    def _():
        @when(line == 3)
        def _():
            for j, s in subs:
                hb[j, rows(s)] = jnp.zeros((depth // SUBS, LANES), f32)
            for j, s in subs:
                f2(mine(j), s).wait_recv()
                agm(mine(j), j, s).start()

        @when(line == 2)
        def _():
            for j in range(2):
                raw(mine(j)).wait_recv()
                for s in range(SUBS):
                    pass_across(j, s, gu[mine(j), rows(s)])

        for j, s in subs:
            f3(0, j, s).wait_recv()
            agt(2 * first + j, j, s).start()

        read_neighbour()

        @when(line == 3)
        def _():
            read_mid()
            take_own()

            @when(left)
            def _():
                for j, s in subs:
                    agb(j, s).wait_recv()
            take_incoming(1 - x, [hx[0], hx[1]])
            send_share(1, kg[...])

        write_att(first, read_state(top, first, gt))

        @when(line == 2)
        def _():
            take_own()
        for j, s in subs:
            agt(2 * (1 - first) + j, j, s).wait_recv()
        total = read_state(top, 1 - first, gt)
        send_share(0, qg[...])
        write_att(1 - first, total)

        @when(line == 2)
        def _():
            take_other()
            send_share(1, kg[...])

    def collect(which, out):
        total = qk_send[which, head]
        for j in range(n_head - 1):
            share(which, j).wait_recv()
            total = total + qk_recv[which, j]
        out[...] = total

    collect(0, qg_out)
    collect(1, kg_out)

    for which in range(2):
        for j in range(n_head - 1):
            share(which, j).wait_send()

    @when(line < 3)
    def _():
        for j, s in subs:
            f1(other(j), s).wait_send()

    @when(jnp.logical_or(line == 0, jnp.logical_and(line < 3, left)))
    def _():
        for j, s in subs:
            f1(mine(j), s).wait_send()

    @when(left, line == 3)
    def _():
        for c in range(chunks):
            for s in range(SUBS):
                f1(c, s).wait_send()

    @when(even)
    def _():
        for j, s in subs:
            f2(mine(j), s).wait_send()

    @when(line == 0)
    def _():
        for j, s in subs:
            f2(other(j), s).wait_send()

    @when(line == 3)
    def _():
        for j, s in subs:
            agm(mine(j), j, s).wait_send()

    @when(odd)
    def _():
        for c in range(chunks):
            raw(c).wait_send()

    @when(line == 1)
    def _():
        for j, s in subs:
            f3(0, j, s).wait_send()
            f3(1, j, s).wait_send()

    @when(late)
    def _():
        for j, s in subs:
            agt(2 * first + j, j, s).wait_send()
        for s in range(SUBS):
            for i in AHEAD:
                b1(i, s).wait_send()
            for d in range(2):
                b2(d, low, s).wait_send()

    @when(jnp.logical_or(right, even))
    def _():
        for j in range(2):
            e1(j).wait_send()

    @when(jnp.logical_or(right, line < 3))
    def _():
        for j, s in subs:
            agb(j, s).wait_send()


def line_scratch(tokens, depth, total_width, code_shape, n_head):
    chunks = total_width // LANES
    rows = tokens // n_head
    f32, bf16 = jnp.float32, jnp.bfloat16
    dma = pltpu.SemaphoreType.DMA

    def states(*lead):
        return pltpu.VMEM((*lead, depth, LANES), f32)

    return {
        "att": pltpu.VMEM((tokens, total_width), f32),
        "vg": pltpu.VMEM((tokens, total_width), f32),
        "qg": pltpu.VMEM((tokens, depth), f32),
        "kg": pltpu.VMEM((tokens, depth), f32),
        "wts": pltpu.VMEM((3, tokens, total_width), bf16),
        "lams": pltpu.VMEM((3, tokens, total_width), bf16),
        **{n: states(chunks) for n in ("own", "sx", "gm", "gt", "w0", "wmid", "wtop", "rr", "gu")},
        **{n: states(2) for n in ("tt", "gz", "es", "g0", "hb", "hs", "hx")},
        "rz": states(3),
        "zz": states(),
        "nearby": pltpu.VMEM((depth, total_width), f32),
        "qk_send": pltpu.VMEM((2, n_head, rows, depth), f32),
        "qk_recv": pltpu.VMEM((2, n_head - 1, rows, depth), f32),
        "q": pltpu.VMEM((tokens, depth), bf16),
        "k": pltpu.VMEM((tokens, depth), bf16),
        "v": pltpu.VMEM((tokens, total_width), bf16),
        "code": pltpu.VMEM((code_shape[1], code_shape[0], tokens), jnp.int32),
        "g": pltpu.VMEM((tokens, total_width), bf16),
        **{n: dma((chunks, SUBS)) for n in ("f1s", "f1r", "f2s", "f2r")},
        **{n: dma((2, SUBS)) for n in (
            "agms", "agmr", "f3r", "agts", "agtr", "b2s", "b2r", "agbs", "agbr")},
        "f3s": dma((2, 2, SUBS)),
        **{n: dma((3, SUBS)) for n in ("b1s", "b1r")},
        **{n: dma((2,)) for n in ("e1s", "e1r")},
        **{n: dma((chunks,)) for n in ("us_", "ur_")},
        **{n: dma((2, n_head - 1)) for n in ("hs_", "hr_")},
        "load": dma((5,)),
        "entry": pltpu.SemaphoreType.REGULAR,
    }


def on_line(n_head, queries, keys, values, level_codes, cotangent):
    tokens, depth = queries.shape
    total_width = values.shape[1]
    rows = tokens // n_head
    f32, bf16 = jnp.float32, jnp.bfloat16
    vmem = pl.BlockSpec(memory_space=pltpu.VMEM)
    scratch = line_scratch(tokens, depth, total_width, level_codes.shape, n_head)
    results = pl.pallas_call(
        functools.partial(line_kernel, n_head, tuple(scratch)),
        out_shape=(
            *[jax.ShapeDtypeStruct((tokens // PIECES, total_width), bf16)] * (2 * PIECES),
            jax.ShapeDtypeStruct((rows, depth), f32),
            jax.ShapeDtypeStruct((rows, depth), f32),
        ),
        in_specs=[pl.BlockSpec(memory_space=pltpu.HBM)] * 5,
        out_specs=(vmem,) * (2 * PIECES + 2),
        scratch_shapes=list(scratch.values()),
        compiler_params=pltpu.CompilerParams(
            collective_id=1, has_side_effects=True, vmem_limit_bytes=ROOM),
    )(queries, keys, values, jnp.transpose(level_codes, (1, 0, 2)), cotangent)
    return hand_over(tokens, total_width, results)


def per_device(n_seq, n_head, queries, keys, values, level_codes, cotangent):
    suits = n_seq == 8 and n_head == 4 and values.shape[1] == 4 * LANES and queries.shape[0] == 2 * STRETCH
    if suits:
        return on_line(n_head, queries, keys, values, level_codes, cotangent)
    return on_any(n_seq, n_head, queries, keys, values, level_codes, cotangent)


def solution(mesh):
    placed = (
        P("seq", None),
        P("seq", None),
        P("seq", "head"),
        P("head", None, "seq"),
        P("seq", "head"),
    )
    return jax.shard_map(
        functools.partial(per_device, mesh.shape["seq"], mesh.shape["head"]),
        mesh=mesh,
        in_specs=placed,
        out_specs=(
            P("seq", "head"),
            P(("seq", "head"), None),
            P(("seq", "head"), None),
            P("seq", "head"),
        ),
        check_vma=False,
    )
```

```python
import functools

import jax
import jax.numpy as jnp
from jax import lax
from jax.experimental import pallas as pl
from jax.experimental.pallas import tpu as pltpu
from jax.sharding import PartitionSpec as P

STRETCH_BITS = 7
STRETCH = 128
LANES = 128
SCALE_CODE = 0.125
MESH = pl.DeviceIdType.MESH
PIECES = 8
ROOM = 54656 * 1024


def dot(a, b, da, db):
    return lax.dot_general(a, b, (((da,), (db,)), ((), ())), preferred_element_type=jnp.float32)


def kernel(
    n_seq, n_head,
    q_in, k_in, v_in, code_in, g_in,
    *rest,
):
    att_outs, vg_outs = rest[:PIECES], rest[PIECES:2 * PIECES]
    (
    qg_out, kg_out,
    att, vg, qg, kg, wts, lams, own, got, pend, back, racc, qk_send, qk_recv,
    f_send, f_recv, b_send, b_recv, h_send, h_recv,
    q_ref, k_ref, v_ref, code_ref, g_ref, load) = rest[2 * PIECES:]
    loads = [
        pltpu.make_async_copy(src, dst, load.at[i])
        for i, (src, dst) in enumerate((
            (k_in, k_ref), (v_in, v_ref), (g_in, g_ref), (q_in, q_ref), (code_in, code_ref)))
    ]
    for one in loads:
        one.start()
    tokens, depth = q_ref.shape
    total_width = v_ref.shape[1]
    heads = code_ref.shape[1]
    width = total_width // heads
    chunks = total_width // LANES
    per_chunk = LANES // width
    blocks = tokens // STRETCH
    rows = tokens // n_head
    bits = n_seq.bit_length() - 1
    scale = depth ** -0.5
    near = STRETCH_BITS + 1
    far = near + 1
    f32, bf16 = jnp.float32, jnp.bfloat16
    seq, head = lax.axis_index("seq"), lax.axis_index("head")
    bit = [lax.rem(lax.div(seq, 1 << b), 2) for b in range(bits)]
    low_bits = bits - 2
    top, mid = bits - 1, bits - 2
    stride = 1 << mid
    line = lax.div(seq, stride)
    partner = [seq + (1 << b) * (1 - 2 * bit[b]) for b in range(low_bits)]
    peers = [lax.rem(head + j, n_head) for j in range(1, n_head)]

    barrier = pltpu.get_barrier_semaphore()

    def greet(to):
        pl.semaphore_signal(barrier, inc=1, device_id=to, device_id_type=MESH)

    for b in range(low_bits):
        greet((partner[b], head))
    for peer in peers:
        greet((seq, peer))

    @pl.when(line > 0)
    def _():
        greet((seq - stride, head))

    @pl.when(line < 3)
    def _():
        greet((seq + stride, head))

    greetings = low_bits + n_head - 1 + (line > 0).astype(jnp.int32) + (line < 3).astype(jnp.int32)

    def forward(b, c, relay=False):
        return pltpu.make_async_remote_copy(
            src_ref=(got if relay else own).at[b, c], dst_ref=got.at[b, c],
            send_sem=f_send.at[b, c], recv_sem=f_recv.at[b, c],
            device_id=(partner[b] if b < low_bits else seq + stride, head), device_id_type=MESH)

    def backward(b, c):
        return pltpu.make_async_remote_copy(
            src_ref=pend.at[b, c], dst_ref=back.at[b, c],
            send_sem=b_send.at[b, c], recv_sem=b_recv.at[b, c],
            device_id=(partner[b] if b < low_bits else seq - stride, head), device_id_type=MESH)

    highest = [lax.div(seq, 2 << b) == (n_seq >> (b + 1)) - 1 for b in range(low_bits)]
    up_sends = [jnp.logical_or(bit[b] == 0, jnp.logical_not(highest[b])) for b in range(low_bits)]
    up_gets = [jnp.logical_or(bit[b] == 1, jnp.logical_not(highest[b])) for b in range(low_bits)]
    down_sends, down_gets = up_gets, up_sends

    cols = [slice(c * LANES, (c + 1) * LANES) for c in range(chunks)]

    spread = (
        lax.broadcasted_iota(jnp.int32, (heads, total_width), 1) // width
        == lax.broadcasted_iota(jnp.int32, (heads, total_width), 0)
    ).astype(f32)

    def level_weights(level):
        lam = code_ref[level].astype(f32) * SCALE_CODE
        return dot(lam, spread, 0, 0)

    def prepare(b):
        @pl.when(bit[b] == 1)
        def _():
            lam = level_weights(far + b)
            lams[b] = lam.astype(bf16)
            weighted = (g_ref[...].astype(f32) * lam).astype(bf16)
            wts[b] = weighted
            sending = dot(q_ref[...], weighted, 0, 0) * scale
            for c in range(chunks):
                pend[b, c] = sending[:, cols[c]]

        if b < low_bits:
            @pl.when(bit[b] == 0)
            def _():
                for c in range(chunks):
                    pend[b, c] = jnp.zeros((depth, LANES), f32)

    first_half = slice(0, STRETCH)
    second_half = slice(STRETCH, 2 * STRETCH)
    loads[0].wait()
    loads[1].wait()
    state_low = dot(k_ref[first_half, :], v_ref[first_half, :], 0, 0)
    state_all = state_low + dot(k_ref[second_half, :], v_ref[second_half, :], 0, 0)
    for c in range(chunks):
        own[0, c] = state_all[:, cols[c]]
    pl.semaphore_wait(barrier, greetings)
    for c in range(chunks):
        @pl.when(up_sends[0])
        def _(c=c):
            forward(0, c).start()
    for one in loads[2:]:
        one.wait()
    prepare(top)
    for c in range(chunks):
        @pl.when(line == 3)
        def _(c=c):
            backward(top, c).start()
    prepare(mid)
    for c in range(chunks):
        @pl.when(line == 3)
        def _(c=c):
            backward(mid, c).start()
    for b in range(low_bits - 1, -1, -1):
        prepare(b)

    key_pos = lax.rem(lax.broadcasted_iota(jnp.int32, (per_chunk * STRETCH, STRETCH), 0), STRETCH)
    query_pos = lax.broadcasted_iota(jnp.int32, (per_chunk * STRETCH, STRETCH), 1)
    differ = jnp.bitwise_xor(query_pos, key_pos)
    causal = key_pos <= query_pos
    lane_head = lax.broadcasted_iota(jnp.int32, (STRETCH, LANES), 1) // width

    def split_heads(block):
        block = block.astype(f32)
        return jnp.concatenate(
            [jnp.where(lane_head == i, block, 0.0) for i in range(per_chunk)], axis=0).astype(bf16)

    press_sum = [jnp.zeros((STRETCH, STRETCH), f32) for _ in range(blocks)]
    scores = []
    for n in range(blocks):
        at = slice(n * STRETCH, (n + 1) * STRETCH)
        one = dot(k_ref[at, :], q_ref[at, :], 1, 1) * scale
        scores.append(jnp.concatenate([one] * per_chunk, axis=0))

    def unit(n, c):
        at = slice(n * STRETCH, (n + 1) * STRETCH)

        def rows_of(level):
            parts = []
            for i in range(per_chunk):
                row = code_ref[level, c * per_chunk + i:c * per_chunk + i + 1, at].astype(f32) * SCALE_CODE
                parts.append(jnp.broadcast_to(row, (STRETCH, STRETCH)))
            return jnp.concatenate(parts, axis=0)

        mask = rows_of(STRETCH_BITS)
        for level in range(STRETCH_BITS - 1, -1, -1):
            mask = jnp.where(differ < (1 << level), rows_of(level), mask)
        mask = jnp.where(causal, mask, 0.0)
        mixed = (scores[n] * mask).astype(bf16)
        v_split = split_heads(v_ref[at, cols[c]])
        g_block = g_ref[at, cols[c]]
        att[at, cols[c]] = dot(mixed, v_split, 0, 0)
        wide = jnp.concatenate(
            [mixed[i * STRETCH:(i + 1) * STRETCH] for i in range(per_chunk)], axis=1)
        vg[at, cols[c]] = dot(wide, split_heads(g_block), 1, 0)
        press = dot(v_split, g_block, 1, 1) * mask
        for i in range(per_chunk):
            press_sum[n] = press_sum[n] + press[i * STRETCH:(i + 1) * STRETCH]

    def finish_block(n):
        at = slice(n * STRETCH, (n + 1) * STRETCH)
        press = press_sum[n].astype(bf16)
        qg[at, :] = dot(press, k_ref[at, :], 0, 0) * scale
        kg[at, :] = dot(press, q_ref[at, :], 1, 0) * scale

    def near_level():
        low = state_low.astype(bf16)
        lam = level_weights(near)[second_half]
        att[second_half, :] = att[second_half, :] + lam * (
            dot(q_ref[second_half, :], low, 1, 0) * scale)
        weighted = (g_ref[second_half, :].astype(f32) * lam).astype(bf16)
        qg[second_half, :] = qg[second_half, :] + dot(weighted, low, 1, 1) * scale
        return dot(q_ref[second_half, :], weighted, 0, 0) * scale

    def consume(b):
        @pl.when(bit[b] == 1)
        def _():
            total = jnp.zeros((tokens, depth), f32)
            for c in range(chunks):
                state = got[b, c].astype(bf16)
                reading = dot(q_ref[...], state, 1, 0) * scale
                att[:, cols[c]] = att[:, cols[c]] + reading * lams[b, :, cols[c]].astype(f32)
                total = total + dot(wts[b, :, cols[c]], state, 1, 1)
            qg[...] = qg[...] + total * scale

    def share(which, j):
        return pltpu.make_async_remote_copy(
            src_ref=qk_send.at[which, peers[j]], dst_ref=qk_recv.at[which, j],
            send_sem=h_send.at[which, j], recv_sem=h_recv.at[which, j],
            device_id=(seq, peers[j]), device_id_type=MESH)

    def send_share(which, grad):
        for i in range(n_head):
            qk_send[which, i] = grad[i * rows:(i + 1) * rows]
        for j in range(n_head - 1):
            share(which, j).start()

    def step_forward(stage, c):
        if stage < low_bits:
            b = stage

            @pl.when(up_gets[b])
            def _():
                forward(b, c).wait_recv()
                own[b + 1, c] = own[b, c] + got[b, c]

            if b + 1 < low_bits:
                @pl.when(up_sends[b + 1])
                def _():
                    forward(b + 1, c).start()
            else:
                @pl.when(bit[mid] == 0)
                def _():
                    forward(mid, c).start()
        elif stage == low_bits:
            @pl.when(bit[mid] == 1)
            def _():
                forward(mid, c).wait_recv()

            @pl.when(line == 1)
            def _():
                own[top, c] = own[mid, c] + got[mid, c]
                forward(top, c).start()
        elif stage == low_bits + 1:
            @pl.when(line == 2)
            def _():
                forward(top, c).wait_recv()
                forward(top, c, True).start()
        else:
            @pl.when(line == 3)
            def _():
                forward(top, c).wait_recv()

    def pass_down(b, c):
        pend[b, c] = pend[b, c] + racc[c]

        @pl.when(down_sends[b])
        def _():
            backward(b, c).start()

    def step_backward(stage, c):
        if stage == 0:
            @pl.when(line == 2)
            def _():
                backward(top, c).wait_recv()
                pend[top, c] = pend[top, c] + back[top, c]
                backward(top, c).start()

            @pl.when(line == 3)
            def _():
                racc[c] = jnp.zeros((depth, LANES), f32)
                pass_down(low_bits - 1, c)
        elif stage == 1:
            @pl.when(line == 1)
            def _():
                backward(top, c).wait_recv()
                pend[mid, c] = pend[mid, c] + back[top, c]
                backward(mid, c).start()
                racc[c] = back[top, c]
                pass_down(low_bits - 1, c)

            @pl.when(line == 2)
            def _():
                backward(mid, c).wait_recv()
                racc[c] = back[mid, c]
                pass_down(low_bits - 1, c)
        elif stage == 2:
            @pl.when(line == 0)
            def _():
                backward(mid, c).wait_recv()
                racc[c] = back[mid, c]
                pass_down(low_bits - 1, c)
        else:
            b = low_bits - 1 - (stage - 3)

            @pl.when(down_gets[b])
            def _():
                backward(b, c).wait_recv()
                racc[c] = racc[c] + back[b, c]

            if b > 0:
                pass_down(b - 1, c)

    near_sum = None
    stages = low_bits + 3
    for c in range(chunks):
        unit(0, c)
    finish_block(0)
    for c in range(chunks):
        step_backward(0, c)
        step_forward(0, c)
    for stage in range(1, low_bits):
        for c in range(chunks):
            step_forward(stage, c)
    for c in range(chunks):
        step_backward(1, c)
        step_forward(low_bits, c)
    for c in range(chunks):
        step_backward(2, c)
        step_forward(low_bits + 1, c)
    for c in range(chunks):
        unit(1, c)
    finish_block(1)
    near_sum = near_level()
    for b in range(low_bits):
        consume(b)
    consume(mid)
    for c in range(chunks):
        step_forward(low_bits + 2, c)
    consume(top)
    send_share(0, qg[...])
    part = tokens // PIECES
    for p in range(PIECES):
        att_outs[p][...] = att[p * part:(p + 1) * part, :].astype(bf16)
    for stage in range(3, stages):
        for c in range(chunks):
            step_backward(stage, c)

    grad_low = kg[first_half, :]
    grad_high = kg[second_half, :]
    for c in range(chunks):
        incoming = racc[c]
        low = (incoming + near_sum[:, cols[c]]).astype(bf16)
        high = incoming.astype(bf16)
        grad_low = grad_low + dot(v_ref[first_half, cols[c]], low, 1, 1)
        grad_high = grad_high + dot(v_ref[second_half, cols[c]], high, 1, 1)
    send_share(1, jnp.concatenate([grad_low, grad_high], axis=0))
    for c in range(chunks):
        incoming = racc[c]
        low = (incoming + near_sum[:, cols[c]]).astype(bf16)
        high = incoming.astype(bf16)
        for half, state in ((first_half, low), (second_half, high)):
            final = (vg[half, cols[c]] + dot(k_ref[half, :], state, 1, 0)).astype(bf16)
            for p in range(PIECES // 2):
                vg_outs[half.start // part + p][:, cols[c]] = final[p * part:(p + 1) * part]

    for which, out in ((0, qg_out), (1, kg_out)):
        total = qk_send[which, head]
        for j in range(n_head - 1):
            share(which, j).wait_recv()
            total = total + qk_recv[which, j]
        out[...] = total
    for which in range(2):
        for j in range(n_head - 1):
            share(which, j).wait_send()
    for c in range(chunks):
        for b in range(low_bits):
            @pl.when(up_sends[b])
            def _(b=b, c=c):
                forward(b, c).wait_send()

            @pl.when(down_sends[b])
            def _(b=b, c=c):
                backward(b, c).wait_send()

        @pl.when(bit[mid] == 0)
        def _(c=c):
            forward(mid, c).wait_send()

        @pl.when(bit[mid] == 1)
        def _(c=c):
            backward(mid, c).wait_send()

        @pl.when(line == 1)
        def _(c=c):
            forward(top, c).wait_send()

        @pl.when(line == 2)
        def _(c=c):
            forward(top, c, True).wait_send()

        @pl.when(line >= 2)
        def _(c=c):
            backward(top, c).wait_send()


def on_any(n_seq, n_head, queries, keys, values, level_codes, cotangent):
    tokens, depth = queries.shape
    total_width = values.shape[1]
    chunks = total_width // LANES
    rows = tokens // n_head
    bits = n_seq.bit_length() - 1
    f32, bf16 = jnp.float32, jnp.bfloat16
    vmem = pl.BlockSpec(memory_space=pltpu.VMEM)
    links = (bits, chunks, depth, LANES)
    dma = pltpu.SemaphoreType.DMA
    results = pl.pallas_call(
        functools.partial(kernel, n_seq, n_head),
        out_shape=(
            *[jax.ShapeDtypeStruct((tokens // PIECES, total_width), bf16)] * (2 * PIECES),
            jax.ShapeDtypeStruct((rows, depth), f32),
            jax.ShapeDtypeStruct((rows, depth), f32),
        ),
        in_specs=[pl.BlockSpec(memory_space=pltpu.HBM)] * 5,
        out_specs=(vmem,) * (2 * PIECES + 2),
        scratch_shapes=[
            pltpu.VMEM((tokens, total_width), f32),
            pltpu.VMEM((tokens, total_width), f32),
            pltpu.VMEM((tokens, depth), f32),
            pltpu.VMEM((tokens, depth), f32),
            pltpu.VMEM((bits, tokens, total_width), bf16),
            pltpu.VMEM((bits, tokens, total_width), bf16),
            pltpu.VMEM(links, f32),
            pltpu.VMEM(links, f32),
            pltpu.VMEM(links, f32),
            pltpu.VMEM(links, f32),
            pltpu.VMEM((chunks, depth, LANES), f32),
            pltpu.VMEM((2, n_head, rows, depth), f32),
            pltpu.VMEM((2, n_head - 1, rows, depth), f32),
            dma((bits, chunks)),
            dma((bits, chunks)),
            dma((bits, chunks)),
            dma((bits, chunks)),
            dma((2, n_head - 1)),
            dma((2, n_head - 1)),
            pltpu.VMEM((tokens, depth), bf16),
            pltpu.VMEM((tokens, depth), bf16),
            pltpu.VMEM((tokens, total_width), bf16),
            pltpu.VMEM((level_codes.shape[1], level_codes.shape[0], tokens), jnp.int32),
            pltpu.VMEM((tokens, total_width), bf16),
            dma((5,)),
        ],
        compiler_params=pltpu.CompilerParams(
            collective_id=0, has_side_effects=True, vmem_limit_bytes=ROOM),
    )(queries, keys, values, jnp.transpose(level_codes, (1, 0, 2)), cotangent)
    return hand_over(tokens, total_width, results)


def settle(*refs):
    att_parts, vg_parts = refs[:PIECES], refs[PIECES:2 * PIECES]
    qg, kg, att_out, qg_out, kg_out, vg_out, sems = refs[2 * PIECES:]
    part = att_parts[0].shape[0]
    pairs = [(qg, qg_out), (kg, kg_out)]
    for p in range(PIECES):
        pairs.append((att_parts[p], att_out.at[pl.ds(p * part, part)]))
        pairs.append((vg_parts[p], vg_out.at[pl.ds(p * part, part)]))
    copies = [pltpu.make_async_copy(a, b, sems.at[i]) for i, (a, b) in enumerate(pairs)]
    for one in copies:
        one.start()
    for one in copies:
        one.wait()


def hand_over(tokens, total_width, results):
    wide = jax.ShapeDtypeStruct((tokens, total_width), jnp.bfloat16)
    thin = jax.ShapeDtypeStruct(results[-1].shape, jnp.float32)
    anywhere = pl.BlockSpec(memory_space=pl.ANY)
    return pl.pallas_call(
        settle,
        out_shape=(wide, thin, thin, wide),
        in_specs=[anywhere] * len(results),
        out_specs=(anywhere,) * 4,
        scratch_shapes=[pltpu.SemaphoreType.DMA((len(results),))],
        compiler_params=pltpu.CompilerParams(vmem_limit_bytes=1024 * 1024),
    )(*results)


SUBS = 2
AHEAD = (3, 2, 1)


def line_kernel(n_head, names, q_in, k_in, v_in, code_in, g_in, *rest):
    att_outs, vg_outs = rest[:PIECES], rest[PIECES:2 * PIECES]
    qg_out, kg_out = rest[2 * PIECES:2 * PIECES + 2]
    r = dict(zip(names, rest[2 * PIECES + 2:]))
    att, vg, qg, kg, wts, lams = (r[n] for n in ("att", "vg", "qg", "kg", "wts", "lams"))
    own, sx, rr, gm, tt, gt = (r[n] for n in ("own", "sx", "rr", "gm", "tt", "gt"))
    w0, wmid, wtop, rz, zz, gz = (r[n] for n in ("w0", "wmid", "wtop", "rz", "zz", "gz"))
    gu, g0, hb, hs, hx = (r[n] for n in ("gu", "g0", "hb", "hs", "hx"))
    es = r["es"]
    nearby, qk_send, qk_recv = (r[n] for n in ("nearby", "qk_send", "qk_recv"))
    q_ref, k_ref, v_ref, code_ref, g_ref = (r[n] for n in ("q", "k", "v", "code", "g"))
    load, entry = r["load"], r["entry"]

    loads = [
        pltpu.make_async_copy(src, dst, load.at[i])
        for i, (src, dst) in enumerate((
            (k_in, k_ref), (v_in, v_ref), (g_in, g_ref), (q_in, q_ref), (code_in, code_ref)))
    ]
    for one in loads:
        one.start()
    tokens, depth = q_ref.shape
    total_width = v_ref.shape[1]
    heads = code_ref.shape[1]
    width = total_width // heads
    chunks = total_width // LANES
    per_chunk = LANES // width
    blocks = tokens // STRETCH
    share_rows = tokens // n_head
    scale = depth ** -0.5
    near = STRETCH_BITS + 1
    far = near + 1
    top, mid = 2, 1
    half_width = total_width // 2
    f32, bf16 = jnp.float32, jnp.bfloat16
    seq, head = lax.axis_index("seq"), lax.axis_index("head")
    x = lax.rem(seq, 2)
    line = lax.div(seq, 2)
    low = lax.rem(line, 2)
    across = seq + 1 - 2 * x
    first = x + low * (1 - 2 * x)
    peers = [lax.rem(head + j, n_head) for j in range(1, n_head)]

    def when(*conditions):
        return pl.when(functools.reduce(jnp.logical_and, conditions))

    left, right = x == 0, x == 1
    early, late = line < 2, line >= 2
    even, odd = low == 0, low == 1
    barrier = pltpu.get_barrier_semaphore()

    def greet(to, sem=barrier):
        pl.semaphore_signal(sem, inc=1, device_id=to, device_id_type=MESH)

    greet((across, head))
    for peer in peers:
        greet((seq, peer))

    @when(line == 0)
    def _():
        greet((seq + 2, head))

    @when(early)
    def _():
        greet((x + 4, head))
        greet((x + 6, head))

    @when(line == 1)
    def _():
        greet((7 - x, head))

    @when(late)
    def _():
        greet((seq + 2 - 4 * low, head))
        greet((across + 2 - 4 * low, head))

    def rows(s):
        return pl.ds(s * (depth // SUBS), depth // SUBS)

    subs = [(j, s) for j in range(2) for s in range(SUBS)]

    def mine(j):
        return 2 * x + j

    def other(j):
        return 2 * (1 - x) + j

    def remote(src, dst, send, recv, to):
        return pltpu.make_async_remote_copy(
            src_ref=src, dst_ref=dst, send_sem=send, recv_sem=recv,
            device_id=(to, head), device_id_type=MESH)

    def f1(c, s):
        return remote(own.at[c, rows(s)], sx.at[c, rows(s)],
                      r["f1s"].at[c, s], r["f1r"].at[c, s], across)

    def f2(c, s):
        return remote(rr.at[c, rows(s)], gm.at[c, rows(s)],
                      r["f2s"].at[c, s], r["f2r"].at[c, s], seq + 2)

    def agm(c, j, s):
        return remote(gm.at[c, rows(s)], gm.at[c, rows(s)],
                      r["agms"].at[j, s], r["agmr"].at[j, s], across)

    def f3(d, j, s):
        return remote(tt.at[j, rows(s)], gt.at[mine(j), rows(s)],
                      r["f3s"].at[d, j, s], r["f3r"].at[j, s], seq + 2 if d == 1 else across + 4)

    def agt(c, j, s):
        return remote(gt.at[c, rows(s)], gt.at[c, rows(s)],
                      r["agts"].at[j, s], r["agtr"].at[j, s], seq + 2 - 4 * low)

    def b1(i, s):
        there_x = x if i % 2 == 0 else 1 - x
        there_low = low if i < 2 else 1 - low
        to = seq + (there_x - x) + 2 * (there_low - low)
        return remote(wtop.at[2 * there_x + there_low, rows(s)], rz.at[i - 1, rows(s)],
                      r["b1s"].at[i - 1, s], r["b1r"].at[i - 1, s], to)

    def b2(d, j, s):
        return remote(zz.at[rows(s)], gz.at[j, rows(s)],
                      r["b2s"].at[d, s], r["b2r"].at[j, s], x + 2 * d)

    def raw(c):
        return remote(wmid.at[c], gu.at[c], r["us_"].at[c], r["ur_"].at[c], seq - 2)

    def e1(j):
        return remote(es.at[j], g0.at[j], r["e1s"].at[j], r["e1r"].at[j], across)

    def agb(j, s):
        return remote(hs.at[j, rows(s)], hx.at[j, rows(s)],
                      r["agbs"].at[j, s], r["agbr"].at[j, s], across)

    def share(which, j):
        return pltpu.make_async_remote_copy(
            src_ref=qk_send.at[which, peers[j]], dst_ref=qk_recv.at[which, j],
            send_sem=r["hs_"].at[which, j], recv_sem=r["hr_"].at[which, j],
            device_id=(seq, peers[j]), device_id_type=MESH)

    def send_share(which, grad):
        for i in range(n_head):
            qk_send[which, i] = grad[i * share_rows:(i + 1) * share_rows]
        for j in (1, 2, 0) if n_head == 4 else range(n_head - 1):
            share(which, j).start()

    cols = [slice(c * LANES, (c + 1) * LANES) for c in range(chunks)]
    spread = (
        lax.broadcasted_iota(jnp.int32, (heads, total_width), 1) // width
        == lax.broadcasted_iota(jnp.int32, (heads, total_width), 0)
    ).astype(f32)

    def level_weights(level):
        lam = code_ref[level].astype(f32) * SCALE_CODE
        return dot(lam, spread, 0, 0)

    def prepare(b, into):
        lam = level_weights(far + b)
        lams[b] = lam.astype(bf16)
        weighted = (g_ref[...].astype(f32) * lam).astype(bf16)
        wts[b] = weighted
        sending = dot(q_ref[...], weighted, 0, 0) * scale
        for c in range(chunks):
            into[c] = sending[:, cols[c]]

    first_half = slice(0, STRETCH)
    second_half = slice(STRETCH, 2 * STRETCH)
    for one in loads:
        one.wait()

    @when(late)
    def _():
        prepare(top, wtop)

        @when(line == 2)
        def _():
            pl.semaphore_wait(barrier, n_head + 4)

        @when(line == 3)
        def _():
            pl.semaphore_wait(barrier, n_head + 5)
        for s in range(SUBS):
            for i in AHEAD:
                b1(i, s).start()
        greet((first + 2, head), entry)

    state_low = dot(k_ref[first_half, :], v_ref[first_half, :], 0, 0)
    state_all = state_low + dot(k_ref[second_half, :], v_ref[second_half, :], 0, 0)
    for c in range(chunks):
        own[c] = state_all[:, cols[c]]

    @when(line == 0)
    def _():
        pl.semaphore_wait(barrier, n_head)

    @when(line == 1)
    def _():
        pl.semaphore_wait(barrier, n_head + 1)
        greet((x, head), entry)

    @when(early)
    def _():
        for j, s in subs:
            f1(other(j), s).start()

    @when(early, jnp.logical_or(line == 0, left))
    def _():
        for j, s in subs:
            f1(mine(j), s).start()

    @when(odd)
    def _():
        prepare(mid, wmid)

    @when(line == 1)
    def _():
        for half in (other, mine):
            for j in range(2):
                raw(half(j)).start()

    @when(right)
    def _():
        prepare(0, w0)

        @when(odd)
        def _():
            for j in range(2):
                es[j] = w0[j]

    key_pos = lax.rem(lax.broadcasted_iota(jnp.int32, (per_chunk * STRETCH, STRETCH), 0), STRETCH)
    query_pos = lax.broadcasted_iota(jnp.int32, (per_chunk * STRETCH, STRETCH), 1)
    differ = jnp.bitwise_xor(query_pos, key_pos)
    causal = key_pos <= query_pos
    lane_head = lax.broadcasted_iota(jnp.int32, (STRETCH, LANES), 1) // width

    def split_heads(block):
        block = block.astype(f32)
        return jnp.concatenate(
            [jnp.where(lane_head == i, block, 0.0) for i in range(per_chunk)], axis=0).astype(bf16)

    def do_block(n):
        at = slice(n * STRETCH, (n + 1) * STRETCH)
        one = dot(k_ref[at, :], q_ref[at, :], 1, 1) * scale
        scores = jnp.concatenate([one] * per_chunk, axis=0)
        press_sum = jnp.zeros((STRETCH, STRETCH), f32)
        for c in range(chunks):
            def rows_of(level):
                parts = []
                for i in range(per_chunk):
                    row = code_ref[level, c * per_chunk + i:c * per_chunk + i + 1, at].astype(f32) * SCALE_CODE
                    parts.append(jnp.broadcast_to(row, (STRETCH, STRETCH)))
                return jnp.concatenate(parts, axis=0)

            mask = rows_of(STRETCH_BITS)
            for level in range(STRETCH_BITS - 1, -1, -1):
                mask = jnp.where(differ < (1 << level), rows_of(level), mask)
            mask = jnp.where(causal, mask, 0.0)
            mixed = (scores * mask).astype(bf16)
            v_split = split_heads(v_ref[at, cols[c]])
            g_block = g_ref[at, cols[c]]
            att[at, cols[c]] = dot(mixed, v_split, 0, 0)
            wide = jnp.concatenate(
                [mixed[i * STRETCH:(i + 1) * STRETCH] for i in range(per_chunk)], axis=1)
            vg[at, cols[c]] = dot(wide, split_heads(g_block), 1, 0)
            press = dot(v_split, g_block, 1, 1) * mask
            for i in range(per_chunk):
                press_sum = press_sum + press[i * STRETCH:(i + 1) * STRETCH]
        press_sum = press_sum.astype(bf16)
        qg[at, :] = dot(press_sum, k_ref[at, :], 0, 0) * scale
        kg[at, :] = dot(press_sum, q_ref[at, :], 1, 0) * scale

    def near_level():
        state = state_low.astype(bf16)
        lam = level_weights(near)[second_half]
        att[second_half, :] = att[second_half, :] + lam * (
            dot(q_ref[second_half, :], state, 1, 0) * scale)
        weighted = (g_ref[second_half, :].astype(f32) * lam).astype(bf16)
        qg[second_half, :] = qg[second_half, :] + dot(weighted, state, 1, 1) * scale
        nearby[...] = dot(q_ref[second_half, :], weighted, 0, 0) * scale

    def span(side):
        return pl.ds(pl.multiple_of(side * half_width, half_width), half_width)

    def read_state(b, side, ref):
        at = span(side)
        state = jnp.concatenate([ref[2 * side], ref[2 * side + 1]], axis=1).astype(bf16)
        reading = dot(q_ref[...], state, 1, 0) * scale
        total = att[:, at] + reading * lams[b, :, at].astype(f32)
        qg[...] = qg[...] + dot(wts[b, :, at], state, 1, 1) * scale
        return total

    def consume(b, side, ref):
        att[:, span(side)] = read_state(b, side, ref)

    part = tokens // PIECES

    def write_att(side, total):
        total = total.astype(bf16)
        for p in range(PIECES):
            att_outs[p][:, span(side)] = total[p * part:(p + 1) * part]

    def take_incoming(side, pair):
        at = span(side)
        incoming = jnp.concatenate(pair, axis=1)
        for half, state in (
                (first_half, incoming + nearby[:, at]), (second_half, incoming)):
            state = state.astype(bf16)
            kg[half, :] = kg[half, :] + dot(v_ref[half, at], state, 1, 1)
            final = (vg[half, at] + dot(k_ref[half, :], state, 1, 0)).astype(bf16)
            for p in range(PIECES // 2):
                vg_outs[half.start // part + p][:, at] = final[p * part:(p + 1) * part]

    do_block(0)

    @when(line == 2)
    def _():
        for j, s in subs:
            f1(other(j), s).start()

    @when(left, line == 2)
    def _():
        for j, s in subs:
            f1(mine(j), s).start()

    @when(left, line == 3)
    def _():
        for half in (0, 2):
            for j, s in subs:
                f1(half + j, s).start()

    @when(line == 3)
    def _():
        for j in range(2):
            raw(other(j)).start()

    @when(right, line == 3)
    def _():
        for j in range(2):
            e1(j).start()

    @when(late)
    def _():
        for s in range(SUBS):
            for i in AHEAD:
                b1(i, s).wait_recv()
            zz[rows(s)] = (wtop[mine(low), rows(s)] + rz[0, rows(s)]) + (
                rz[1, rows(s)] + rz[2, rows(s)])
            b2(0, low, s).start()
        for s in range(SUBS):
            b2(1, low, s).start()

    @when(line == 0)
    def _():
        pl.semaphore_wait(entry, 1)

    def add_near(j, s):
        f1(mine(j), s).wait_recv()
        rr[mine(j), rows(s)] = own[mine(j), rows(s)] + sx[mine(j), rows(s)]

    @when(early)
    def _():
        for j, s in subs:
            add_near(j, s)

            @when(line == 0)
            def _():
                f2(mine(j), s).start()

    @when(line == 3)
    def _():
        for j in range(2):
            raw(mine(j)).start()

        @when(right)
        def _():
            for j, s in subs:
                hs[j, rows(s)] = w0[2 + j, rows(s)]
                hx[j, rows(s)] = jnp.zeros((depth // SUBS, LANES), f32)
                agb(j, s).start()

    @when(right, line == 1)
    def _():
        for j in range(2):
            e1(j).start()

    do_block(1)
    near_level()

    @when(line == 1)
    def _():
        pl.semaphore_wait(entry, 2)
        for j, s in subs:
            f2(mine(j), s).wait_recv()
            tt[j, rows(s)] = gm[mine(j), rows(s)] + rr[mine(j), rows(s)]
            f3(0, j, s).start()
            f3(1, j, s).start()

    def pass_raw():
        for j in range(2):
            raw(other(j)).wait_recv()

            @when(left)
            def _():
                es[j] = gu[2 + j]

            @when(right)
            def _():
                es[j] = gu[j] + w0[j]
            e1(j).start()

    @when(line == 0)
    def _():
        pass_raw()

    @when(line == 2)
    def _():
        for j, s in subs:
            add_near(j, s)
            f2(mine(j), s).start()

    @when(line == 0)
    def _():
        for j, s in subs:
            f1(other(j), s).wait_recv()
            rr[other(j), rows(s)] = own[other(j), rows(s)] + sx[other(j), rows(s)]
            f2(other(j), s).start()

    @when(line == 2)
    def _():
        pass_raw()

    def read_neighbour():
        @when(right, jnp.logical_or(line == 1, line == 2))
        def _():
            for j, s in subs:
                f1(j, s).wait_recv()

        @when(right, line == 3)
        def _():
            for c in range(chunks):
                for s in range(SUBS):
                    f1(c, s).wait_recv()

        @when(right)
        def _():
            consume(0, 0, sx)
            consume(0, 1, sx)

    def read_mid():
        @when(line == 1)
        def _():
            for j, s in subs:
                f2(other(j), s).wait_recv()

        @when(line == 3)
        def _():
            for j, s in subs:
                agm(other(j), j, s).wait_recv()
        consume(mid, 0, gm)
        consume(mid, 1, gm)

    def pass_across(j, s, total):
        hb[j, rows(s)] = total

        @when(left)
        def _():
            hs[j, rows(s)] = total

        @when(right)
        def _():
            hs[j, rows(s)] = total + w0[2 + j, rows(s)]

        agb(j, s).start()

    def take_own():
        @when(jnp.logical_or(left, even))
        def _():
            for j in range(2):
                e1(j).wait_recv()
                hb[j] = hb[j] + g0[j]
        take_incoming(x, [hb[0], hb[1]])

    def take_other():
        for j, s in subs:
            agb(j, s).wait_recv()

        @when(even)
        def _():
            for j in range(2):
                hx[j] = hx[j] + gu[other(j)]
        take_incoming(1 - x, [hx[0], hx[1]])

    @when(early)
    def _():
        read_neighbour()

        @when(line == 1)
        def _():
            read_mid()

        send_share(0, qg[...])
        write_att(0, att[:, :half_width])
        write_att(1, att[:, half_width:])

        @when(line == 0)
        def _():
            for j in range(2):
                raw(mine(j)).wait_recv()
        for j, s in subs:
            b2(0, j, s).wait_recv()

            @when(line == 0)
            def _():
                gz[j, rows(s)] = gz[j, rows(s)] + gu[mine(j), rows(s)]
            pass_across(j, s, gz[j, rows(s)])
        take_own()
        take_other()
        send_share(1, kg[...])

    @when(late)
    def _():
        @when(line == 3)
        def _():
            for j, s in subs:
                hb[j, rows(s)] = jnp.zeros((depth // SUBS, LANES), f32)
            for j, s in subs:
                f2(mine(j), s).wait_recv()
                agm(mine(j), j, s).start()

        @when(line == 2)
        def _():
            for j in range(2):
                raw(mine(j)).wait_recv()
                for s in range(SUBS):
                    pass_across(j, s, gu[mine(j), rows(s)])

        for j, s in subs:
            f3(0, j, s).wait_recv()
            agt(2 * first + j, j, s).start()

        read_neighbour()

        @when(line == 3)
        def _():
            read_mid()
            take_own()

            @when(left)
            def _():
                for j, s in subs:
                    agb(j, s).wait_recv()
            take_incoming(1 - x, [hx[0], hx[1]])
            send_share(1, kg[...])

        write_att(first, read_state(top, first, gt))

        @when(line == 2)
        def _():
            take_own()
        for j, s in subs:
            agt(2 * (1 - first) + j, j, s).wait_recv()
        total = read_state(top, 1 - first, gt)
        send_share(0, qg[...])
        write_att(1 - first, total)

        @when(line == 2)
        def _():
            take_other()
            send_share(1, kg[...])

    def collect(which, out):
        total = qk_send[which, head]
        for j in range(n_head - 1):
            share(which, j).wait_recv()
            total = total + qk_recv[which, j]
        out[...] = total

    collect(0, qg_out)
    collect(1, kg_out)

    for which in range(2):
        for j in range(n_head - 1):
            share(which, j).wait_send()

    @when(line < 3)
    def _():
        for j, s in subs:
            f1(other(j), s).wait_send()

    @when(jnp.logical_or(line == 0, jnp.logical_and(line < 3, left)))
    def _():
        for j, s in subs:
            f1(mine(j), s).wait_send()

    @when(left, line == 3)
    def _():
        for c in range(chunks):
            for s in range(SUBS):
                f1(c, s).wait_send()

    @when(even)
    def _():
        for j, s in subs:
            f2(mine(j), s).wait_send()

    @when(line == 0)
    def _():
        for j, s in subs:
            f2(other(j), s).wait_send()

    @when(line == 3)
    def _():
        for j, s in subs:
            agm(mine(j), j, s).wait_send()

    @when(odd)
    def _():
        for c in range(chunks):
            raw(c).wait_send()

    @when(line == 1)
    def _():
        for j, s in subs:
            f3(0, j, s).wait_send()
            f3(1, j, s).wait_send()

    @when(late)
    def _():
        for j, s in subs:
            agt(2 * first + j, j, s).wait_send()
        for s in range(SUBS):
            for i in AHEAD:
                b1(i, s).wait_send()
            for d in range(2):
                b2(d, low, s).wait_send()

    @when(jnp.logical_or(right, even))
    def _():
        for j in range(2):
            e1(j).wait_send()

    @when(jnp.logical_or(right, line < 3))
    def _():
        for j, s in subs:
            agb(j, s).wait_send()


def line_scratch(tokens, depth, total_width, code_shape, n_head):
    chunks = total_width // LANES
    rows = tokens // n_head
    f32, bf16 = jnp.float32, jnp.bfloat16
    dma = pltpu.SemaphoreType.DMA

    def states(*lead):
        return pltpu.VMEM((*lead, depth, LANES), f32)

    return {
        "att": pltpu.VMEM((tokens, total_width), f32),
        "vg": pltpu.VMEM((tokens, total_width), f32),
        "qg": pltpu.VMEM((tokens, depth), f32),
        "kg": pltpu.VMEM((tokens, depth), f32),
        "wts": pltpu.VMEM((3, tokens, total_width), bf16),
        "lams": pltpu.VMEM((3, tokens, total_width), bf16),
        **{n: states(chunks) for n in ("own", "sx", "gm", "gt", "w0", "wmid", "wtop", "rr", "gu")},
        **{n: states(2) for n in ("tt", "gz", "es", "g0", "hb", "hs", "hx")},
        "rz": states(3),
        "zz": states(),
        "nearby": pltpu.VMEM((depth, total_width), f32),
        "qk_send": pltpu.VMEM((2, n_head, rows, depth), f32),
        "qk_recv": pltpu.VMEM((2, n_head - 1, rows, depth), f32),
        "q": pltpu.VMEM((tokens, depth), bf16),
        "k": pltpu.VMEM((tokens, depth), bf16),
        "v": pltpu.VMEM((tokens, total_width), bf16),
        "code": pltpu.VMEM((code_shape[1], code_shape[0], tokens), jnp.int32),
        "g": pltpu.VMEM((tokens, total_width), bf16),
        **{n: dma((chunks, SUBS)) for n in ("f1s", "f1r", "f2s", "f2r")},
        **{n: dma((2, SUBS)) for n in (
            "agms", "agmr", "f3r", "agts", "agtr", "b2s", "b2r", "agbs", "agbr")},
        "f3s": dma((2, 2, SUBS)),
        **{n: dma((3, SUBS)) for n in ("b1s", "b1r")},
        **{n: dma((2,)) for n in ("e1s", "e1r")},
        **{n: dma((chunks,)) for n in ("us_", "ur_")},
        **{n: dma((2, n_head - 1)) for n in ("hs_", "hr_")},
        "load": dma((5,)),
        "entry": pltpu.SemaphoreType.REGULAR,
    }


def on_line(n_head, queries, keys, values, level_codes, cotangent):
    tokens, depth = queries.shape
    total_width = values.shape[1]
    rows = tokens // n_head
    f32, bf16 = jnp.float32, jnp.bfloat16
    vmem = pl.BlockSpec(memory_space=pltpu.VMEM)
    scratch = line_scratch(tokens, depth, total_width, level_codes.shape, n_head)
    results = pl.pallas_call(
        functools.partial(line_kernel, n_head, tuple(scratch)),
        out_shape=(
            *[jax.ShapeDtypeStruct((tokens // PIECES, total_width), bf16)] * (2 * PIECES),
            jax.ShapeDtypeStruct((rows, depth), f32),
            jax.ShapeDtypeStruct((rows, depth), f32),
        ),
        in_specs=[pl.BlockSpec(memory_space=pltpu.HBM)] * 5,
        out_specs=(vmem,) * (2 * PIECES + 2),
        scratch_shapes=list(scratch.values()),
        compiler_params=pltpu.CompilerParams(
            collective_id=1, has_side_effects=True, vmem_limit_bytes=ROOM),
    )(queries, keys, values, jnp.transpose(level_codes, (1, 0, 2)), cotangent)
    return hand_over(tokens, total_width, results)


def per_device(n_seq, n_head, queries, keys, values, level_codes, cotangent):
    suits = n_seq == 8 and n_head == 4 and values.shape[1] == 4 * LANES and queries.shape[0] == 2 * STRETCH
    if suits:
        return on_line(n_head, queries, keys, values, level_codes, cotangent)
    return on_any(n_seq, n_head, queries, keys, values, level_codes, cotangent)


def solution(mesh):
    placed = (
        P("seq", None),
        P("seq", None),
        P("seq", "head"),
        P("head", None, "seq"),
        P("seq", "head"),
    )
    return jax.shard_map(
        functools.partial(per_device, mesh.shape["seq"], mesh.shape["head"]),
        mesh=mesh,
        in_specs=placed,
        out_specs=(
            P("seq", "head"),
            P(("seq", "head"), None),
            P(("seq", "head"), None),
            P("seq", "head"),
        ),
        check_vma=False,
    )
```

```python
import functools

import jax
import jax.numpy as jnp
from jax import lax
from jax.experimental import pallas as pl
from jax.experimental.pallas import tpu as pltpu
from jax.sharding import PartitionSpec as P

STRETCH_BITS = 7
STRETCH = 128
LANES = 128
SCALE_CODE = 0.125
MESH = pl.DeviceIdType.MESH
PIECES = 8
ROOM = 54656 * 1024


def dot(a, b, da, db):
    return lax.dot_general(a, b, (((da,), (db,)), ((), ())), preferred_element_type=jnp.float32)


def kernel(
    n_seq, n_head,
    q_in, k_in, v_in, code_in, g_in,
    *rest,
):
    att_outs, vg_outs = rest[:PIECES], rest[PIECES:2 * PIECES]
    (
    qg_out, kg_out,
    att, vg, qg, kg, wts, lams, own, got, pend, back, racc, qk_send, qk_recv,
    f_send, f_recv, b_send, b_recv, h_send, h_recv,
    q_ref, k_ref, v_ref, code_ref, g_ref, load) = rest[2 * PIECES:]
    loads = [
        pltpu.make_async_copy(src, dst, load.at[i])
        for i, (src, dst) in enumerate((
            (k_in, k_ref), (v_in, v_ref), (g_in, g_ref), (q_in, q_ref), (code_in, code_ref)))
    ]
    for one in loads:
        one.start()
    tokens, depth = q_ref.shape
    total_width = v_ref.shape[1]
    heads = code_ref.shape[1]
    width = total_width // heads
    chunks = total_width // LANES
    per_chunk = LANES // width
    blocks = tokens // STRETCH
    rows = tokens // n_head
    bits = n_seq.bit_length() - 1
    scale = depth ** -0.5
    near = STRETCH_BITS + 1
    far = near + 1
    f32, bf16 = jnp.float32, jnp.bfloat16
    seq, head = lax.axis_index("seq"), lax.axis_index("head")
    bit = [lax.rem(lax.div(seq, 1 << b), 2) for b in range(bits)]
    low_bits = bits - 2
    top, mid = bits - 1, bits - 2
    stride = 1 << mid
    line = lax.div(seq, stride)
    partner = [seq + (1 << b) * (1 - 2 * bit[b]) for b in range(low_bits)]
    peers = [lax.rem(head + j, n_head) for j in range(1, n_head)]

    barrier = pltpu.get_barrier_semaphore()

    def greet(to):
        pl.semaphore_signal(barrier, inc=1, device_id=to, device_id_type=MESH)

    for b in range(low_bits):
        greet((partner[b], head))
    for peer in peers:
        greet((seq, peer))

    @pl.when(line > 0)
    def _():
        greet((seq - stride, head))

    @pl.when(line < 3)
    def _():
        greet((seq + stride, head))

    greetings = low_bits + n_head - 1 + (line > 0).astype(jnp.int32) + (line < 3).astype(jnp.int32)

    def forward(b, c, relay=False):
        return pltpu.make_async_remote_copy(
            src_ref=(got if relay else own).at[b, c], dst_ref=got.at[b, c],
            send_sem=f_send.at[b, c], recv_sem=f_recv.at[b, c],
            device_id=(partner[b] if b < low_bits else seq + stride, head), device_id_type=MESH)

    def backward(b, c):
        return pltpu.make_async_remote_copy(
            src_ref=pend.at[b, c], dst_ref=back.at[b, c],
            send_sem=b_send.at[b, c], recv_sem=b_recv.at[b, c],
            device_id=(partner[b] if b < low_bits else seq - stride, head), device_id_type=MESH)

    highest = [lax.div(seq, 2 << b) == (n_seq >> (b + 1)) - 1 for b in range(low_bits)]
    up_sends = [jnp.logical_or(bit[b] == 0, jnp.logical_not(highest[b])) for b in range(low_bits)]
    up_gets = [jnp.logical_or(bit[b] == 1, jnp.logical_not(highest[b])) for b in range(low_bits)]
    down_sends, down_gets = up_gets, up_sends

    cols = [slice(c * LANES, (c + 1) * LANES) for c in range(chunks)]

    spread = (
        lax.broadcasted_iota(jnp.int32, (heads, total_width), 1) // width
        == lax.broadcasted_iota(jnp.int32, (heads, total_width), 0)
    ).astype(f32)

    def level_weights(level):
        lam = code_ref[level].astype(f32) * SCALE_CODE
        return dot(lam, spread, 0, 0)

    def prepare(b):
        @pl.when(bit[b] == 1)
        def _():
            lam = level_weights(far + b)
            lams[b] = lam.astype(bf16)
            weighted = (g_ref[...].astype(f32) * lam).astype(bf16)
            wts[b] = weighted
            sending = dot(q_ref[...], weighted, 0, 0) * scale
            for c in range(chunks):
                pend[b, c] = sending[:, cols[c]]

        if b < low_bits:
            @pl.when(bit[b] == 0)
            def _():
                for c in range(chunks):
                    pend[b, c] = jnp.zeros((depth, LANES), f32)

    first_half = slice(0, STRETCH)
    second_half = slice(STRETCH, 2 * STRETCH)
    loads[0].wait()
    loads[1].wait()
    state_low = dot(k_ref[first_half, :], v_ref[first_half, :], 0, 0)
    state_all = state_low + dot(k_ref[second_half, :], v_ref[second_half, :], 0, 0)
    for c in range(chunks):
        own[0, c] = state_all[:, cols[c]]
    pl.semaphore_wait(barrier, greetings)
    for c in range(chunks):
        @pl.when(up_sends[0])
        def _(c=c):
            forward(0, c).start()
    for one in loads[2:]:
        one.wait()
    prepare(top)
    for c in range(chunks):
        @pl.when(line == 3)
        def _(c=c):
            backward(top, c).start()
    prepare(mid)
    for c in range(chunks):
        @pl.when(line == 3)
        def _(c=c):
            backward(mid, c).start()
    for b in range(low_bits - 1, -1, -1):
        prepare(b)

    key_pos = lax.rem(lax.broadcasted_iota(jnp.int32, (per_chunk * STRETCH, STRETCH), 0), STRETCH)
    query_pos = lax.broadcasted_iota(jnp.int32, (per_chunk * STRETCH, STRETCH), 1)
    differ = jnp.bitwise_xor(query_pos, key_pos)
    causal = key_pos <= query_pos
    lane_head = lax.broadcasted_iota(jnp.int32, (STRETCH, LANES), 1) // width

    def split_heads(block):
        block = block.astype(f32)
        return jnp.concatenate(
            [jnp.where(lane_head == i, block, 0.0) for i in range(per_chunk)], axis=0).astype(bf16)

    press_sum = [jnp.zeros((STRETCH, STRETCH), f32) for _ in range(blocks)]
    scores = []
    for n in range(blocks):
        at = slice(n * STRETCH, (n + 1) * STRETCH)
        one = dot(k_ref[at, :], q_ref[at, :], 1, 1) * scale
        scores.append(jnp.concatenate([one] * per_chunk, axis=0))

    def unit(n, c):
        at = slice(n * STRETCH, (n + 1) * STRETCH)

        def rows_of(level):
            parts = []
            for i in range(per_chunk):
                row = code_ref[level, c * per_chunk + i:c * per_chunk + i + 1, at].astype(f32) * SCALE_CODE
                parts.append(jnp.broadcast_to(row, (STRETCH, STRETCH)))
            return jnp.concatenate(parts, axis=0)

        mask = rows_of(STRETCH_BITS)
        for level in range(STRETCH_BITS - 1, -1, -1):
            mask = jnp.where(differ < (1 << level), rows_of(level), mask)
        mask = jnp.where(causal, mask, 0.0)
        mixed = (scores[n] * mask).astype(bf16)
        v_split = split_heads(v_ref[at, cols[c]])
        g_block = g_ref[at, cols[c]]
        att[at, cols[c]] = dot(mixed, v_split, 0, 0)
        wide = jnp.concatenate(
            [mixed[i * STRETCH:(i + 1) * STRETCH] for i in range(per_chunk)], axis=1)
        vg[at, cols[c]] = dot(wide, split_heads(g_block), 1, 0)
        press = dot(v_split, g_block, 1, 1) * mask
        for i in range(per_chunk):
            press_sum[n] = press_sum[n] + press[i * STRETCH:(i + 1) * STRETCH]

    def finish_block(n):
        at = slice(n * STRETCH, (n + 1) * STRETCH)
        press = press_sum[n].astype(bf16)
        qg[at, :] = dot(press, k_ref[at, :], 0, 0) * scale
        kg[at, :] = dot(press, q_ref[at, :], 1, 0) * scale

    def near_level():
        low = state_low.astype(bf16)
        lam = level_weights(near)[second_half]
        att[second_half, :] = att[second_half, :] + lam * (
            dot(q_ref[second_half, :], low, 1, 0) * scale)
        weighted = (g_ref[second_half, :].astype(f32) * lam).astype(bf16)
        qg[second_half, :] = qg[second_half, :] + dot(weighted, low, 1, 1) * scale
        return dot(q_ref[second_half, :], weighted, 0, 0) * scale

    def consume(b):
        @pl.when(bit[b] == 1)
        def _():
            total = jnp.zeros((tokens, depth), f32)
            for c in range(chunks):
                state = got[b, c].astype(bf16)
                reading = dot(q_ref[...], state, 1, 0) * scale
                att[:, cols[c]] = att[:, cols[c]] + reading * lams[b, :, cols[c]].astype(f32)
                total = total + dot(wts[b, :, cols[c]], state, 1, 1)
            qg[...] = qg[...] + total * scale

    def share(which, j):
        return pltpu.make_async_remote_copy(
            src_ref=qk_send.at[which, peers[j]], dst_ref=qk_recv.at[which, j],
            send_sem=h_send.at[which, j], recv_sem=h_recv.at[which, j],
            device_id=(seq, peers[j]), device_id_type=MESH)

    def send_share(which, grad):
        for i in range(n_head):
            qk_send[which, i] = grad[i * rows:(i + 1) * rows]
        for j in range(n_head - 1):
            share(which, j).start()

    def step_forward(stage, c):
        if stage < low_bits:
            b = stage

            @pl.when(up_gets[b])
            def _():
                forward(b, c).wait_recv()
                own[b + 1, c] = own[b, c] + got[b, c]

            if b + 1 < low_bits:
                @pl.when(up_sends[b + 1])
                def _():
                    forward(b + 1, c).start()
            else:
                @pl.when(bit[mid] == 0)
                def _():
                    forward(mid, c).start()
        elif stage == low_bits:
            @pl.when(bit[mid] == 1)
            def _():
                forward(mid, c).wait_recv()

            @pl.when(line == 1)
            def _():
                own[top, c] = own[mid, c] + got[mid, c]
                forward(top, c).start()
        elif stage == low_bits + 1:
            @pl.when(line == 2)
            def _():
                forward(top, c).wait_recv()
                forward(top, c, True).start()
        else:
            @pl.when(line == 3)
            def _():
                forward(top, c).wait_recv()

    def pass_down(b, c):
        pend[b, c] = pend[b, c] + racc[c]

        @pl.when(down_sends[b])
        def _():
            backward(b, c).start()

    def step_backward(stage, c):
        if stage == 0:
            @pl.when(line == 2)
            def _():
                backward(top, c).wait_recv()
                pend[top, c] = pend[top, c] + back[top, c]
                backward(top, c).start()

            @pl.when(line == 3)
            def _():
                racc[c] = jnp.zeros((depth, LANES), f32)
                pass_down(low_bits - 1, c)
        elif stage == 1:
            @pl.when(line == 1)
            def _():
                backward(top, c).wait_recv()
                pend[mid, c] = pend[mid, c] + back[top, c]
                backward(mid, c).start()
                racc[c] = back[top, c]
                pass_down(low_bits - 1, c)

            @pl.when(line == 2)
            def _():
                backward(mid, c).wait_recv()
                racc[c] = back[mid, c]
                pass_down(low_bits - 1, c)
        elif stage == 2:
            @pl.when(line == 0)
            def _():
                backward(mid, c).wait_recv()
                racc[c] = back[mid, c]
                pass_down(low_bits - 1, c)
        else:
            b = low_bits - 1 - (stage - 3)

            @pl.when(down_gets[b])
            def _():
                backward(b, c).wait_recv()
                racc[c] = racc[c] + back[b, c]

            if b > 0:
                pass_down(b - 1, c)

    near_sum = None
    stages = low_bits + 3
    for c in range(chunks):
        unit(0, c)
    finish_block(0)
    for c in range(chunks):
        step_backward(0, c)
        step_forward(0, c)
    for stage in range(1, low_bits):
        for c in range(chunks):
            step_forward(stage, c)
    for c in range(chunks):
        step_backward(1, c)
        step_forward(low_bits, c)
    for c in range(chunks):
        step_backward(2, c)
        step_forward(low_bits + 1, c)
    for c in range(chunks):
        unit(1, c)
    finish_block(1)
    near_sum = near_level()
    for b in range(low_bits):
        consume(b)
    consume(mid)
    for c in range(chunks):
        step_forward(low_bits + 2, c)
    consume(top)
    send_share(0, qg[...])
    part = tokens // PIECES
    for p in range(PIECES):
        att_outs[p][...] = att[p * part:(p + 1) * part, :].astype(bf16)
    for stage in range(3, stages):
        for c in range(chunks):
            step_backward(stage, c)

    grad_low = kg[first_half, :]
    grad_high = kg[second_half, :]
    for c in range(chunks):
        incoming = racc[c]
        low = (incoming + near_sum[:, cols[c]]).astype(bf16)
        high = incoming.astype(bf16)
        grad_low = grad_low + dot(v_ref[first_half, cols[c]], low, 1, 1)
        grad_high = grad_high + dot(v_ref[second_half, cols[c]], high, 1, 1)
    send_share(1, jnp.concatenate([grad_low, grad_high], axis=0))
    for c in range(chunks):
        incoming = racc[c]
        low = (incoming + near_sum[:, cols[c]]).astype(bf16)
        high = incoming.astype(bf16)
        for half, state in ((first_half, low), (second_half, high)):
            final = (vg[half, cols[c]] + dot(k_ref[half, :], state, 1, 0)).astype(bf16)
            for p in range(PIECES // 2):
                vg_outs[half.start // part + p][:, cols[c]] = final[p * part:(p + 1) * part]

    for which, out in ((0, qg_out), (1, kg_out)):
        total = qk_send[which, head]
        for j in range(n_head - 1):
            share(which, j).wait_recv()
            total = total + qk_recv[which, j]
        out[...] = total
    for which in range(2):
        for j in range(n_head - 1):
            share(which, j).wait_send()
    for c in range(chunks):
        for b in range(low_bits):
            @pl.when(up_sends[b])
            def _(b=b, c=c):
                forward(b, c).wait_send()

            @pl.when(down_sends[b])
            def _(b=b, c=c):
                backward(b, c).wait_send()

        @pl.when(bit[mid] == 0)
        def _(c=c):
            forward(mid, c).wait_send()

        @pl.when(bit[mid] == 1)
        def _(c=c):
            backward(mid, c).wait_send()

        @pl.when(line == 1)
        def _(c=c):
            forward(top, c).wait_send()

        @pl.when(line == 2)
        def _(c=c):
            forward(top, c, True).wait_send()

        @pl.when(line >= 2)
        def _(c=c):
            backward(top, c).wait_send()


def on_any(n_seq, n_head, queries, keys, values, level_codes, cotangent):
    tokens, depth = queries.shape
    total_width = values.shape[1]
    chunks = total_width // LANES
    rows = tokens // n_head
    bits = n_seq.bit_length() - 1
    f32, bf16 = jnp.float32, jnp.bfloat16
    vmem = pl.BlockSpec(memory_space=pltpu.VMEM)
    links = (bits, chunks, depth, LANES)
    dma = pltpu.SemaphoreType.DMA
    results = pl.pallas_call(
        functools.partial(kernel, n_seq, n_head),
        out_shape=(
            *[jax.ShapeDtypeStruct((tokens // PIECES, total_width), bf16)] * (2 * PIECES),
            jax.ShapeDtypeStruct((rows, depth), f32),
            jax.ShapeDtypeStruct((rows, depth), f32),
        ),
        in_specs=[pl.BlockSpec(memory_space=pltpu.HBM)] * 5,
        out_specs=(vmem,) * (2 * PIECES + 2),
        scratch_shapes=[
            pltpu.VMEM((tokens, total_width), f32),
            pltpu.VMEM((tokens, total_width), f32),
            pltpu.VMEM((tokens, depth), f32),
            pltpu.VMEM((tokens, depth), f32),
            pltpu.VMEM((bits, tokens, total_width), bf16),
            pltpu.VMEM((bits, tokens, total_width), bf16),
            pltpu.VMEM(links, f32),
            pltpu.VMEM(links, f32),
            pltpu.VMEM(links, f32),
            pltpu.VMEM(links, f32),
            pltpu.VMEM((chunks, depth, LANES), f32),
            pltpu.VMEM((2, n_head, rows, depth), f32),
            pltpu.VMEM((2, n_head - 1, rows, depth), f32),
            dma((bits, chunks)),
            dma((bits, chunks)),
            dma((bits, chunks)),
            dma((bits, chunks)),
            dma((2, n_head - 1)),
            dma((2, n_head - 1)),
            pltpu.VMEM((tokens, depth), bf16),
            pltpu.VMEM((tokens, depth), bf16),
            pltpu.VMEM((tokens, total_width), bf16),
            pltpu.VMEM((level_codes.shape[1], level_codes.shape[0], tokens), jnp.int32),
            pltpu.VMEM((tokens, total_width), bf16),
            dma((5,)),
        ],
        compiler_params=pltpu.CompilerParams(
            collective_id=0, has_side_effects=True, vmem_limit_bytes=ROOM),
    )(queries, keys, values, jnp.transpose(level_codes, (1, 0, 2)), cotangent)
    return hand_over(tokens, total_width, results)


def settle(*refs):
    att_parts, vg_parts = refs[:PIECES], refs[PIECES:2 * PIECES]
    qg, kg, att_out, qg_out, kg_out, vg_out, sems = refs[2 * PIECES:]
    part = att_parts[0].shape[0]
    pairs = [(qg, qg_out), (kg, kg_out)]
    for p in range(PIECES):
        pairs.append((att_parts[p], att_out.at[pl.ds(p * part, part)]))
        pairs.append((vg_parts[p], vg_out.at[pl.ds(p * part, part)]))
    copies = [pltpu.make_async_copy(a, b, sems.at[i]) for i, (a, b) in enumerate(pairs)]
    for one in copies:
        one.start()
    for one in copies:
        one.wait()


def hand_over(tokens, total_width, results):
    wide = jax.ShapeDtypeStruct((tokens, total_width), jnp.bfloat16)
    thin = jax.ShapeDtypeStruct(results[-1].shape, jnp.float32)
    anywhere = pl.BlockSpec(memory_space=pl.ANY)
    return pl.pallas_call(
        settle,
        out_shape=(wide, thin, thin, wide),
        in_specs=[anywhere] * len(results),
        out_specs=(anywhere,) * 4,
        scratch_shapes=[pltpu.SemaphoreType.DMA((len(results),))],
        compiler_params=pltpu.CompilerParams(vmem_limit_bytes=1024 * 1024),
    )(*results)


SUBS = 2
AHEAD = (3, 2, 1)


def line_kernel(n_head, names, q_in, k_in, v_in, code_in, g_in, *rest):
    att_outs, vg_outs = rest[:PIECES], rest[PIECES:2 * PIECES]
    qg_out, kg_out = rest[2 * PIECES:2 * PIECES + 2]
    r = dict(zip(names, rest[2 * PIECES + 2:]))
    att, vg, qg, kg, wts, lams = (r[n] for n in ("att", "vg", "qg", "kg", "wts", "lams"))
    own, sx, rr, gm, tt, gt = (r[n] for n in ("own", "sx", "rr", "gm", "tt", "gt"))
    w0, wmid, wtop, rz, zz, gz = (r[n] for n in ("w0", "wmid", "wtop", "rz", "zz", "gz"))
    gu, g0, hb, hs, hx = (r[n] for n in ("gu", "g0", "hb", "hs", "hx"))
    es = r["es"]
    nearby, qk_send, qk_recv = (r[n] for n in ("nearby", "qk_send", "qk_recv"))
    q_ref, k_ref, v_ref, code_ref, g_ref = (r[n] for n in ("q", "k", "v", "code", "g"))
    load, entry = r["load"], r["entry"]

    loads = [
        pltpu.make_async_copy(src, dst, load.at[i])
        for i, (src, dst) in enumerate((
            (k_in, k_ref), (v_in, v_ref), (g_in, g_ref), (q_in, q_ref), (code_in, code_ref)))
    ]
    for one in loads:
        one.start()
    tokens, depth = q_ref.shape
    total_width = v_ref.shape[1]
    heads = code_ref.shape[1]
    width = total_width // heads
    chunks = total_width // LANES
    per_chunk = LANES // width
    blocks = tokens // STRETCH
    share_rows = tokens // n_head
    scale = depth ** -0.5
    near = STRETCH_BITS + 1
    far = near + 1
    top, mid = 2, 1
    half_width = total_width // 2
    f32, bf16 = jnp.float32, jnp.bfloat16
    seq, head = lax.axis_index("seq"), lax.axis_index("head")
    x = lax.rem(seq, 2)
    line = lax.div(seq, 2)
    low = lax.rem(line, 2)
    across = seq + 1 - 2 * x
    first = x + low * (1 - 2 * x)
    peers = [lax.rem(head + j, n_head) for j in range(1, n_head)]

    def when(*conditions):
        return pl.when(functools.reduce(jnp.logical_and, conditions))

    left, right = x == 0, x == 1
    early, late = line < 2, line >= 2
    even, odd = low == 0, low == 1
    barrier = pltpu.get_barrier_semaphore()

    def greet(to, sem=barrier):
        pl.semaphore_signal(sem, inc=1, device_id=to, device_id_type=MESH)

    greet((across, head))
    for peer in peers:
        greet((seq, peer))

    @when(line == 0)
    def _():
        greet((seq + 2, head))

    @when(early)
    def _():
        greet((x + 4, head))
        greet((x + 6, head))

    @when(line == 1)
    def _():
        greet((7 - x, head))

    @when(late)
    def _():
        greet((seq + 2 - 4 * low, head))
        greet((across + 2 - 4 * low, head))

    def rows(s):
        return pl.ds(s * (depth // SUBS), depth // SUBS)

    subs = [(j, s) for j in range(2) for s in range(SUBS)]

    def mine(j):
        return 2 * x + j

    def other(j):
        return 2 * (1 - x) + j

    def remote(src, dst, send, recv, to):
        return pltpu.make_async_remote_copy(
            src_ref=src, dst_ref=dst, send_sem=send, recv_sem=recv,
            device_id=(to, head), device_id_type=MESH)

    def f1(c, s):
        return remote(own.at[c, rows(s)], sx.at[c, rows(s)],
                      r["f1s"].at[c, s], r["f1r"].at[c, s], across)

    def f2(c, s):
        return remote(rr.at[c, rows(s)], gm.at[c, rows(s)],
                      r["f2s"].at[c, s], r["f2r"].at[c, s], seq + 2)

    def agm(c, j, s):
        return remote(gm.at[c, rows(s)], gm.at[c, rows(s)],
                      r["agms"].at[j, s], r["agmr"].at[j, s], across)

    def f3(d, j, s):
        return remote(tt.at[j, rows(s)], gt.at[mine(j), rows(s)],
                      r["f3s"].at[d, j, s], r["f3r"].at[j, s], seq + 2 if d == 1 else across + 4)

    def agt(c, j, s):
        return remote(gt.at[c, rows(s)], gt.at[c, rows(s)],
                      r["agts"].at[j, s], r["agtr"].at[j, s], seq + 2 - 4 * low)

    def b1(i, s):
        there_x = x if i % 2 == 0 else 1 - x
        there_low = low if i < 2 else 1 - low
        to = seq + (there_x - x) + 2 * (there_low - low)
        return remote(wtop.at[2 * there_x + there_low, rows(s)], rz.at[i - 1, rows(s)],
                      r["b1s"].at[i - 1, s], r["b1r"].at[i - 1, s], to)

    def b2(d, j, s):
        return remote(zz.at[rows(s)], gz.at[j, rows(s)],
                      r["b2s"].at[d, s], r["b2r"].at[j, s], x + 2 * d)

    def raw(c):
        return remote(wmid.at[c], gu.at[c], r["us_"].at[c], r["ur_"].at[c], seq - 2)

    def e1(j):
        return remote(es.at[j], g0.at[j], r["e1s"].at[j], r["e1r"].at[j], across)

    def agb(j, s):
        return remote(hs.at[j, rows(s)], hx.at[j, rows(s)],
                      r["agbs"].at[j, s], r["agbr"].at[j, s], across)

    def share(which, j):
        return pltpu.make_async_remote_copy(
            src_ref=qk_send.at[which, peers[j]], dst_ref=qk_recv.at[which, j],
            send_sem=r["hs_"].at[which, j], recv_sem=r["hr_"].at[which, j],
            device_id=(seq, peers[j]), device_id_type=MESH)

    def send_share(which, grad):
        for i in range(n_head):
            qk_send[which, i] = grad[i * share_rows:(i + 1) * share_rows]
        for j in (1, 2, 0) if n_head == 4 else range(n_head - 1):
            share(which, j).start()

    cols = [slice(c * LANES, (c + 1) * LANES) for c in range(chunks)]
    spread = (
        lax.broadcasted_iota(jnp.int32, (heads, total_width), 1) // width
        == lax.broadcasted_iota(jnp.int32, (heads, total_width), 0)
    ).astype(f32)

    def level_weights(level):
        lam = code_ref[level].astype(f32) * SCALE_CODE
        return dot(lam, spread, 0, 0)

    def prepare(b, into):
        lam = level_weights(far + b)
        lams[b] = lam.astype(bf16)
        weighted = (g_ref[...].astype(f32) * lam).astype(bf16)
        wts[b] = weighted
        sending = dot(q_ref[...], weighted, 0, 0) * scale
        for c in range(chunks):
            into[c] = sending[:, cols[c]]

    first_half = slice(0, STRETCH)
    second_half = slice(STRETCH, 2 * STRETCH)
    for one in loads:
        one.wait()

    @when(late)
    def _():
        prepare(top, wtop)

        @when(line == 2)
        def _():
            pl.semaphore_wait(barrier, n_head + 4)

        @when(line == 3)
        def _():
            pl.semaphore_wait(barrier, n_head + 5)
        for s in range(SUBS):
            for i in AHEAD:
                b1(i, s).start()
        greet((first + 2, head), entry)

    state_low = dot(k_ref[first_half, :], v_ref[first_half, :], 0, 0)
    state_all = state_low + dot(k_ref[second_half, :], v_ref[second_half, :], 0, 0)
    for c in range(chunks):
        own[c] = state_all[:, cols[c]]

    @when(line == 0)
    def _():
        pl.semaphore_wait(barrier, n_head)

    @when(line == 1)
    def _():
        pl.semaphore_wait(barrier, n_head + 1)
        greet((x, head), entry)

    @when(early)
    def _():
        for j, s in subs:
            f1(other(j), s).start()

    @when(early, jnp.logical_or(line == 0, left))
    def _():
        for j, s in subs:
            f1(mine(j), s).start()

    @when(odd)
    def _():
        prepare(mid, wmid)

    @when(line == 1)
    def _():
        for half in (other, mine):
            for j in range(2):
                raw(half(j)).start()

    @when(right)
    def _():
        prepare(0, w0)

        @when(odd)
        def _():
            for j in range(2):
                es[j] = w0[j]

    key_pos = lax.rem(lax.broadcasted_iota(jnp.int32, (per_chunk * STRETCH, STRETCH), 0), STRETCH)
    query_pos = lax.broadcasted_iota(jnp.int32, (per_chunk * STRETCH, STRETCH), 1)
    differ = jnp.bitwise_xor(query_pos, key_pos)
    causal = key_pos <= query_pos
    lane_head = lax.broadcasted_iota(jnp.int32, (STRETCH, LANES), 1) // width

    def split_heads(block):
        block = block.astype(f32)
        return jnp.concatenate(
            [jnp.where(lane_head == i, block, 0.0) for i in range(per_chunk)], axis=0).astype(bf16)

    def do_block(n):
        at = slice(n * STRETCH, (n + 1) * STRETCH)
        one = dot(k_ref[at, :], q_ref[at, :], 1, 1) * scale
        scores = jnp.concatenate([one] * per_chunk, axis=0)
        press_sum = jnp.zeros((STRETCH, STRETCH), f32)
        for c in range(chunks):
            def rows_of(level):
                parts = []
                for i in range(per_chunk):
                    row = code_ref[level, c * per_chunk + i:c * per_chunk + i + 1, at].astype(f32) * SCALE_CODE
                    parts.append(jnp.broadcast_to(row, (STRETCH, STRETCH)))
                return jnp.concatenate(parts, axis=0)

            mask = rows_of(STRETCH_BITS)
            for level in range(STRETCH_BITS - 1, -1, -1):
                mask = jnp.where(differ < (1 << level), rows_of(level), mask)
            mask = jnp.where(causal, mask, 0.0)
            mixed = (scores * mask).astype(bf16)
            v_split = split_heads(v_ref[at, cols[c]])
            g_block = g_ref[at, cols[c]]
            att[at, cols[c]] = dot(mixed, v_split, 0, 0)
            wide = jnp.concatenate(
                [mixed[i * STRETCH:(i + 1) * STRETCH] for i in range(per_chunk)], axis=1)
            vg[at, cols[c]] = dot(wide, split_heads(g_block), 1, 0)
            press = dot(v_split, g_block, 1, 1) * mask
            for i in range(per_chunk):
                press_sum = press_sum + press[i * STRETCH:(i + 1) * STRETCH]
        press_sum = press_sum.astype(bf16)
        qg[at, :] = dot(press_sum, k_ref[at, :], 0, 0) * scale
        kg[at, :] = dot(press_sum, q_ref[at, :], 1, 0) * scale

    def near_level():
        state = state_low.astype(bf16)
        lam = level_weights(near)[second_half]
        att[second_half, :] = att[second_half, :] + lam * (
            dot(q_ref[second_half, :], state, 1, 0) * scale)
        weighted = (g_ref[second_half, :].astype(f32) * lam).astype(bf16)
        qg[second_half, :] = qg[second_half, :] + dot(weighted, state, 1, 1) * scale
        nearby[...] = dot(q_ref[second_half, :], weighted, 0, 0) * scale

    def span(side):
        return pl.ds(pl.multiple_of(side * half_width, half_width), half_width)

    def read_state(b, side, ref):
        at = span(side)
        state = jnp.concatenate([ref[2 * side], ref[2 * side + 1]], axis=1).astype(bf16)
        reading = dot(q_ref[...], state, 1, 0) * scale
        total = att[:, at] + reading * lams[b, :, at].astype(f32)
        qg[...] = qg[...] + dot(wts[b, :, at], state, 1, 1) * scale
        return total

    def consume(b, side, ref):
        att[:, span(side)] = read_state(b, side, ref)

    part = tokens // PIECES

    def write_att(side, total):
        total = total.astype(bf16)
        for p in range(PIECES):
            att_outs[p][:, span(side)] = total[p * part:(p + 1) * part]

    def take_incoming(side, pair):
        at = span(side)
        incoming = jnp.concatenate(pair, axis=1)
        for half, state in (
                (first_half, incoming + nearby[:, at]), (second_half, incoming)):
            state = state.astype(bf16)
            kg[half, :] = kg[half, :] + dot(v_ref[half, at], state, 1, 1)
            final = (vg[half, at] + dot(k_ref[half, :], state, 1, 0)).astype(bf16)
            for p in range(PIECES // 2):
                vg_outs[half.start // part + p][:, at] = final[p * part:(p + 1) * part]

    do_block(0)

    @when(line == 2)
    def _():
        for j, s in subs:
            f1(other(j), s).start()

    @when(left, line == 2)
    def _():
        for j, s in subs:
            f1(mine(j), s).start()

    @when(left, line == 3)
    def _():
        for half in (0, 2):
            for j, s in subs:
                f1(half + j, s).start()

    @when(line == 3)
    def _():
        for j in range(2):
            raw(other(j)).start()

    @when(right, line == 3)
    def _():
        for j in range(2):
            e1(j).start()

    @when(late)
    def _():
        for s in range(SUBS):
            for i in AHEAD:
                b1(i, s).wait_recv()
            zz[rows(s)] = (wtop[mine(low), rows(s)] + rz[0, rows(s)]) + (
                rz[1, rows(s)] + rz[2, rows(s)])
            b2(0, low, s).start()
        for s in range(SUBS):
            b2(1, low, s).start()

    @when(line == 0)
    def _():
        pl.semaphore_wait(entry, 1)

    def add_near(j, s):
        f1(mine(j), s).wait_recv()
        rr[mine(j), rows(s)] = own[mine(j), rows(s)] + sx[mine(j), rows(s)]

    @when(early)
    def _():
        for j, s in subs:
            add_near(j, s)

            @when(line == 0)
            def _():
                f2(mine(j), s).start()

    @when(line == 3)
    def _():
        for j in range(2):
            raw(mine(j)).start()

        @when(right)
        def _():
            for j, s in subs:
                hs[j, rows(s)] = w0[2 + j, rows(s)]
                hx[j, rows(s)] = jnp.zeros((depth // SUBS, LANES), f32)
                agb(j, s).start()

    @when(right, line == 1)
    def _():
        for j in range(2):
            e1(j).start()

    do_block(1)
    near_level()

    @when(line == 1)
    def _():
        pl.semaphore_wait(entry, 2)
        for j, s in subs:
            f2(mine(j), s).wait_recv()
            tt[j, rows(s)] = gm[mine(j), rows(s)] + rr[mine(j), rows(s)]
            f3(0, j, s).start()
            f3(1, j, s).start()

    def pass_raw():
        for j in range(2):
            raw(other(j)).wait_recv()

            @when(left)
            def _():
                es[j] = gu[2 + j]

            @when(right)
            def _():
                es[j] = gu[j] + w0[j]
            e1(j).start()

    @when(line == 0)
    def _():
        pass_raw()

    @when(line == 2)
    def _():
        for j, s in subs:
            add_near(j, s)
            f2(mine(j), s).start()

    @when(line == 0)
    def _():
        for j, s in subs:
            f1(other(j), s).wait_recv()
            rr[other(j), rows(s)] = own[other(j), rows(s)] + sx[other(j), rows(s)]
            f2(other(j), s).start()

    @when(line == 2)
    def _():
        pass_raw()

    def read_neighbour():
        @when(right, jnp.logical_or(line == 1, line == 2))
        def _():
            for j, s in subs:
                f1(j, s).wait_recv()

        @when(right, line == 3)
        def _():
            for c in range(chunks):
                for s in range(SUBS):
                    f1(c, s).wait_recv()

        @when(right)
        def _():
            consume(0, 0, sx)
            consume(0, 1, sx)

    def read_mid():
        @when(line == 1)
        def _():
            for j, s in subs:
                f2(other(j), s).wait_recv()

        @when(line == 3)
        def _():
            for j, s in subs:
                agm(other(j), j, s).wait_recv()
        consume(mid, 0, gm)
        consume(mid, 1, gm)

    def pass_across(j, s, total):
        hb[j, rows(s)] = total

        @when(left)
        def _():
            hs[j, rows(s)] = total

        @when(right)
        def _():
            hs[j, rows(s)] = total + w0[2 + j, rows(s)]

        agb(j, s).start()

    def take_own():
        @when(jnp.logical_or(left, even))
        def _():
            for j in range(2):
                e1(j).wait_recv()
                hb[j] = hb[j] + g0[j]
        take_incoming(x, [hb[0], hb[1]])

    def take_other():
        for j, s in subs:
            agb(j, s).wait_recv()

        @when(even)
        def _():
            for j in range(2):
                hx[j] = hx[j] + gu[other(j)]
        take_incoming(1 - x, [hx[0], hx[1]])

    @when(early)
    def _():
        read_neighbour()

        @when(line == 1)
        def _():
            read_mid()

        send_share(0, qg[...])
        write_att(0, att[:, :half_width])
        write_att(1, att[:, half_width:])

        @when(line == 0)
        def _():
            for j in range(2):
                raw(mine(j)).wait_recv()
        for j, s in subs:
            b2(0, j, s).wait_recv()

            @when(line == 0)
            def _():
                gz[j, rows(s)] = gz[j, rows(s)] + gu[mine(j), rows(s)]
            pass_across(j, s, gz[j, rows(s)])
        take_own()
        take_other()
        send_share(1, kg[...])

    @when(late)
    def _():
        @when(line == 3)
        def _():
            for j, s in subs:
                hb[j, rows(s)] = jnp.zeros((depth // SUBS, LANES), f32)

        @when(line == 2)
        def _():
            for j in range(2):
                raw(mine(j)).wait_recv()
                for s in range(SUBS):
                    pass_across(j, s, gu[mine(j), rows(s)])

        for j, s in subs:
            f3(0, j, s).wait_recv()
            agt(2 * first + j, j, s).start()

        @when(line == 3)
        def _():
            for j, s in subs:
                f2(mine(j), s).wait_recv()
                agm(mine(j), j, s).start()
            take_own()

            @when(left)
            def _():
                for j, s in subs:
                    agb(j, s).wait_recv()
            take_incoming(1 - x, [hx[0], hx[1]])
            send_share(1, kg[...])

        read_neighbour()

        @when(line == 3)
        def _():
            read_mid()

        write_att(first, read_state(top, first, gt))

        @when(line == 2)
        def _():
            take_own()
        for j, s in subs:
            agt(2 * (1 - first) + j, j, s).wait_recv()
        total = read_state(top, 1 - first, gt)
        send_share(0, qg[...])
        write_att(1 - first, total)

        @when(line == 2)
        def _():
            take_other()
            send_share(1, kg[...])

    def collect(which, out):
        total = qk_send[which, head]
        for j in range(n_head - 1):
            share(which, j).wait_recv()
            total = total + qk_recv[which, j]
        out[...] = total

    collect(0, qg_out)
    collect(1, kg_out)

    for which in range(2):
        for j in range(n_head - 1):
            share(which, j).wait_send()

    @when(line < 3)
    def _():
        for j, s in subs:
            f1(other(j), s).wait_send()

    @when(jnp.logical_or(line == 0, jnp.logical_and(line < 3, left)))
    def _():
        for j, s in subs:
            f1(mine(j), s).wait_send()

    @when(left, line == 3)
    def _():
        for c in range(chunks):
            for s in range(SUBS):
                f1(c, s).wait_send()

    @when(even)
    def _():
        for j, s in subs:
            f2(mine(j), s).wait_send()

    @when(line == 0)
    def _():
        for j, s in subs:
            f2(other(j), s).wait_send()

    @when(line == 3)
    def _():
        for j, s in subs:
            agm(mine(j), j, s).wait_send()

    @when(odd)
    def _():
        for c in range(chunks):
            raw(c).wait_send()

    @when(line == 1)
    def _():
        for j, s in subs:
            f3(0, j, s).wait_send()
            f3(1, j, s).wait_send()

    @when(late)
    def _():
        for j, s in subs:
            agt(2 * first + j, j, s).wait_send()
        for s in range(SUBS):
            for i in AHEAD:
                b1(i, s).wait_send()
            for d in range(2):
                b2(d, low, s).wait_send()

    @when(jnp.logical_or(right, even))
    def _():
        for j in range(2):
            e1(j).wait_send()

    @when(jnp.logical_or(right, line < 3))
    def _():
        for j, s in subs:
            agb(j, s).wait_send()


def line_scratch(tokens, depth, total_width, code_shape, n_head):
    chunks = total_width // LANES
    rows = tokens // n_head
    f32, bf16 = jnp.float32, jnp.bfloat16
    dma = pltpu.SemaphoreType.DMA

    def states(*lead):
        return pltpu.VMEM((*lead, depth, LANES), f32)

    return {
        "att": pltpu.VMEM((tokens, total_width), f32),
        "vg": pltpu.VMEM((tokens, total_width), f32),
        "qg": pltpu.VMEM((tokens, depth), f32),
        "kg": pltpu.VMEM((tokens, depth), f32),
        "wts": pltpu.VMEM((3, tokens, total_width), bf16),
        "lams": pltpu.VMEM((3, tokens, total_width), bf16),
        **{n: states(chunks) for n in ("own", "sx", "gm", "gt", "w0", "wmid", "wtop", "rr", "gu")},
        **{n: states(2) for n in ("tt", "gz", "es", "g0", "hb", "hs", "hx")},
        "rz": states(3),
        "zz": states(),
        "nearby": pltpu.VMEM((depth, total_width), f32),
        "qk_send": pltpu.VMEM((2, n_head, rows, depth), f32),
        "qk_recv": pltpu.VMEM((2, n_head - 1, rows, depth), f32),
        "q": pltpu.VMEM((tokens, depth), bf16),
        "k": pltpu.VMEM((tokens, depth), bf16),
        "v": pltpu.VMEM((tokens, total_width), bf16),
        "code": pltpu.VMEM((code_shape[1], code_shape[0], tokens), jnp.int32),
        "g": pltpu.VMEM((tokens, total_width), bf16),
        **{n: dma((chunks, SUBS)) for n in ("f1s", "f1r", "f2s", "f2r")},
        **{n: dma((2, SUBS)) for n in (
            "agms", "agmr", "f3r", "agts", "agtr", "b2s", "b2r", "agbs", "agbr")},
        "f3s": dma((2, 2, SUBS)),
        **{n: dma((3, SUBS)) for n in ("b1s", "b1r")},
        **{n: dma((2,)) for n in ("e1s", "e1r")},
        **{n: dma((chunks,)) for n in ("us_", "ur_")},
        **{n: dma((2, n_head - 1)) for n in ("hs_", "hr_")},
        "load": dma((5,)),
        "entry": pltpu.SemaphoreType.REGULAR,
    }


def on_line(n_head, queries, keys, values, level_codes, cotangent):
    tokens, depth = queries.shape
    total_width = values.shape[1]
    rows = tokens // n_head
    f32, bf16 = jnp.float32, jnp.bfloat16
    vmem = pl.BlockSpec(memory_space=pltpu.VMEM)
    scratch = line_scratch(tokens, depth, total_width, level_codes.shape, n_head)
    results = pl.pallas_call(
        functools.partial(line_kernel, n_head, tuple(scratch)),
        out_shape=(
            *[jax.ShapeDtypeStruct((tokens // PIECES, total_width), bf16)] * (2 * PIECES),
            jax.ShapeDtypeStruct((rows, depth), f32),
            jax.ShapeDtypeStruct((rows, depth), f32),
        ),
        in_specs=[pl.BlockSpec(memory_space=pltpu.HBM)] * 5,
        out_specs=(vmem,) * (2 * PIECES + 2),
        scratch_shapes=list(scratch.values()),
        compiler_params=pltpu.CompilerParams(
            collective_id=1, has_side_effects=True, vmem_limit_bytes=ROOM),
    )(queries, keys, values, jnp.transpose(level_codes, (1, 0, 2)), cotangent)
    return hand_over(tokens, total_width, results)


def per_device(n_seq, n_head, queries, keys, values, level_codes, cotangent):
    suits = n_seq == 8 and n_head == 4 and values.shape[1] == 4 * LANES and queries.shape[0] == 2 * STRETCH
    if suits:
        return on_line(n_head, queries, keys, values, level_codes, cotangent)
    return on_any(n_seq, n_head, queries, keys, values, level_codes, cotangent)


def solution(mesh):
    placed = (
        P("seq", None),
        P("seq", None),
        P("seq", "head"),
        P("head", None, "seq"),
        P("seq", "head"),
    )
    return jax.shard_map(
        functools.partial(per_device, mesh.shape["seq"], mesh.shape["head"]),
        mesh=mesh,
        in_specs=placed,
        out_specs=(
            P("seq", "head"),
            P(("seq", "head"), None),
            P(("seq", "head"), None),
            P("seq", "head"),
        ),
        check_vma=False,
    )
```
